32 devices in a mesh: ctx: 16 (over z, y, x), tp: 2 (over core).
Axes of the slice: x: 2, y: 2, z: 4, core: 2. Of those that a mesh axis runs over, the one named last changes fastest.
Arguments:
- stretch_order: int32 [16], replicated, may hold values from 0 to 15, as said below
- attn_queries: bfloat16 [2048, 4096], P('ctx', 'tp'), may hold values from -4.6 to 4.6
- attn_keys: bfloat16 [2048, 1024], P('ctx', 'tp'), may hold values from -4.6 to 4.6
- attn_values: bfloat16 [2048, 1024], P('ctx', 'tp'), may hold values from -6 to 6
- attn_grad: bfloat16 [2048, 4096], P('ctx', 'tp'), may hold values from -6 to 6
- mamba_input: bfloat16 [2048, 4096], P('ctx', 'tp'), may hold values from -21 to 21
- gate_input: bfloat16 [2048, 4096], P('ctx', 'tp'), may hold values from -6 to 6
- state_write: bfloat16 [2048, 1024], P('ctx', 'tp'), may hold values from -6 to 6
- state_read: bfloat16 [2048, 1024], P('ctx', 'tp'), may hold values from -0.5 to 0.5
- step_raw: float32 [2048, 64], P('ctx', 'tp'), may hold values from -8 to 2
- decay_log: float32 [64], P('tp')
- skip_gain: float32 [64], P('tp'), may hold values from 0.5 to 1.5
- norm_gain: float32 [4096], P('tp'), may hold values from 0.25 to 1.75
- mamba_grad: bfloat16 [2048, 4096], P('ctx', 'tp'), may hold values from -6 to 6
Outputs:
- attn_output: bfloat16 [2048, 4096], P('ctx', 'tp')
- query_grad: bfloat16 [2048, 4096], P('ctx', 'tp')
- mamba_output: bfloat16 [2048, 4096], P('ctx', 'tp')
- input_grad: bfloat16 [2048, 4096], P('ctx', 'tp')
- write_grad: bfloat16 [2048, 1024], P('ctx', 'tp')
- read_grad: bfloat16 [2048, 1024], P('ctx', 'tp')
The draws below stay inside these ranges and needn't reach their ends.
Inputs may be any that keep to these rules, and one draw needn't show every extreme that they name: `stretch_order`: entry i is (i + s) mod 16 for one s of each draw.
All inputs are finite; a program needn't handle non-finite values.
Results may differ from the reference program's by a relative error of at most 0.015.
Values may be sent and summed in bfloat16 or wider, within the bound.
No kernel may reach another device: no remote copies, remote signals or barrier semaphores. Data moves between devices by JAX's collectives and lax.ppermute only.
A program may use at most 128 MiB of HBM per device.

```python
import math
import jax
import jax.numpy as jnp
from jax import lax

TOK_DEV = 128
STRETCH = 64
PAIRS = 16
TOKEN_COUNT = 2048
MAMBA_HEAD_HALF = 64
MDIM = 64
NSTATE = 128
GROUPS = 8
AHEADS = 32
KVHEADS = 8
AHD = 128


def draw_stretch_order(key, part):
    offset_draw = jax.random.randint(jax.random.fold_in(key, 3), (), 0, PAIRS)
    return ((jnp.arange(PAIRS, dtype=jnp.int32) + offset_draw) % PAIRS).astype(jnp.int32)


def attention_pair(key):
    random_base_key = jax.random.fold_in(key, 17)
    query_key, keys_key = jax.random.split(random_base_key, 2)
    queries = jnp.clip(jax.random.normal(query_key, (PAIRS, TOK_DEV, AHEADS, AHD), jnp.float32), -4.5, 4.5)
    keys_drawn = jnp.clip(jax.random.normal(keys_key, (PAIRS, TOK_DEV, KVHEADS, AHD), jnp.float32), -4.5, 4.5)
    return (queries.reshape(TOKEN_COUNT, AHEADS * AHD), keys_drawn.reshape(TOKEN_COUNT, KVHEADS * AHD))


def draw_attn_queries(key, part):
    return attention_pair(key)[0].astype(jnp.bfloat16)


def draw_attn_keys(key, part):
    return attention_pair(key)[1].astype(jnp.bfloat16)


def spike_plan(key):
    random_base_key, random_rows_key, spike_random_key = jax.random.split(jax.random.fold_in(key, 41), 3)
    spike_row_index = jax.random.randint(random_rows_key, (4,), 0, TOKEN_COUNT)
    spike_value_draws = jax.random.uniform(spike_random_key, (4, MAMBA_HEAD_HALF), jnp.float32, 0.5, 2.0)
    return (random_base_key, spike_row_index, spike_value_draws)


def spike_damping(key):
    spike_row_index = spike_plan(key)[1]
    marked_rows = jnp.zeros((TOKEN_COUNT,), jnp.float32).at[spike_row_index].set(1.0)
    return 1.0 - 0.99 * marked_rows


def draw_mamba_input(key, part):
    random_base_key = jax.random.fold_in(jax.random.fold_in(key, 29), 0)
    head_of = jnp.arange(MAMBA_HEAD_HALF * MDIM) // MDIM
    column_scale = jnp.exp(math.log(3.0) * head_of.astype(jnp.float32) / max(MAMBA_HEAD_HALF - 1, 1))
    damping = spike_damping(key)[:, None]
    sampled_values = jnp.clip(jax.random.normal(random_base_key, (TOKEN_COUNT, MAMBA_HEAD_HALF * MDIM), jnp.float32), -4.0, 4.0)
    return (sampled_values * column_scale[None] * damping).astype(jnp.bfloat16)


def draw_state_write(key, part):
    random_base_key = jax.random.fold_in(key, 67)
    damping = spike_damping(key)[:, None]
    sampled_values = jnp.clip(jax.random.normal(random_base_key, (TOKEN_COUNT, GROUPS * NSTATE), jnp.float32), -6.0, 6.0)
    return (sampled_values * damping).astype(jnp.bfloat16)


def draw_step_raw(key, part):
    random_base_key, spike_row_index, spike_value_draws = spike_plan(key)
    sampled_values = jnp.clip(-7.0 + 0.5 * jax.random.normal(random_base_key, (TOKEN_COUNT, MAMBA_HEAD_HALF), jnp.float32), -8.0, -6.0)
    return sampled_values.at[spike_row_index].set(spike_value_draws)


def draw_decay_log(key, part):
    pick_key, fast_key, slow_key = jax.random.split(jax.random.fold_in(key, 53), 3)
    share = 0.5
    fast_heads = jax.random.uniform(pick_key, (MAMBA_HEAD_HALF,), jnp.float32) < share
    fast_log = math.log(25.0) + jax.random.uniform(fast_key, (MAMBA_HEAD_HALF,), jnp.float32, -0.4, 0.4)
    slow_log = math.log(1.2 / (0.0009 * TOKEN_COUNT)) + jax.random.uniform(slow_key, (MAMBA_HEAD_HALF,), jnp.float32, -0.3, 0.3)
    return jnp.where(fast_heads, fast_log, slow_log)


def shard_levels(own_key, extent, shards, smallest, largest):
    gain = 1.0
    for dim, shards_of in shards:
        heights = jax.random.uniform(jax.random.fold_in(jax.random.fold_in(own_key, 6), dim), (shards_of,), jnp.float32, smallest / len(shards), largest / len(shards))
        gain = gain * jnp.repeat(jnp.exp(heights), extent[dim] // shards_of).reshape((-1,) + (1,) * (len(extent) - 1 - dim))
    return gain


def scatter_about(stream_key, shape, scale, most, cuts=(), kind=jnp.bfloat16):
    loudness = shard_levels(stream_key, shape, cuts, -0.22, 0.18) if cuts else 1.0
    values = jax.random.normal(stream_key, shape, jnp.float32) * scale * loudness
    return jnp.minimum(jnp.maximum(values, -most), most).astype(kind)


def setup_inputs(seed: int = 0) -> dict:
    seeds = jax.random.split(jax.random.key(seed), 15)
    return {
        "stretch_order": draw_stretch_order(jax.random.fold_in(seeds[14], 71), 0),
        "attn_queries": draw_attn_queries(jax.random.fold_in(seeds[14], 71), 0),
        "attn_keys": draw_attn_keys(jax.random.fold_in(seeds[14], 71), 0),
        "attn_values": scatter_about(seeds[3], (TOKEN_COUNT, KVHEADS * AHD), 1.0, 6.0, ((0, 16), (1, 2))),
        "attn_grad": scatter_about(seeds[4], (TOKEN_COUNT, AHEADS * AHD), 1.0, 6.0, ((0, 16), (1, 2))),
        "mamba_input": draw_mamba_input(jax.random.fold_in(seeds[14], 71), 0),
        "gate_input": scatter_about(seeds[6], (TOKEN_COUNT, MAMBA_HEAD_HALF * MDIM), 1.0, 6.0, ((0, 16), (1, 2))),
        "state_write": draw_state_write(jax.random.fold_in(seeds[14], 71), 0),
        "state_read": scatter_about(seeds[8], (TOKEN_COUNT, GROUPS * NSTATE), NSTATE ** -0.5, 0.5, ((0, 16), (1, 2))),
        "step_raw": draw_step_raw(jax.random.fold_in(seeds[14], 71), 0),
        "decay_log": draw_decay_log(jax.random.fold_in(seeds[14], 71), 0),
        "skip_gain": jnp.clip(0.5 + 1.0 * jax.random.uniform(seeds[11], (MAMBA_HEAD_HALF,), jnp.float32) ** shard_levels(seeds[11], (MAMBA_HEAD_HALF,), ((0, 2),), -0.2, 0.2), 0.5, 1.5),
        "norm_gain": jnp.clip(1.0 + 0.15 * jax.random.normal(seeds[12], (MAMBA_HEAD_HALF * MDIM,), jnp.float32), 0.25, 1.75),
        "mamba_grad": scatter_about(seeds[13], (TOKEN_COUNT, MAMBA_HEAD_HALF * MDIM), 1.0, 6.0, ((0, 16), (1, 2))),
    }


def stretch_parts(input_rows, write_rows, read_rows, rate_rows, decay_rate, skip_rate):
    length = input_rows.shape[0]
    cumlog = jnp.cumsum(rate_rows * decay_rate[None], axis=0)
    scores = jnp.einsum('tgn,sgn->gts', read_rows, write_rows, preferred_element_type=jnp.float32)
    position = jnp.arange(length)
    causal = position[:, None] >= position[None, :]
    levels = jnp.transpose(cumlog, (1, 2, 0))
    spread = levels[:, :, :, None] - levels[:, :, None, :]
    decays = jnp.where(causal, jnp.exp(jnp.where(causal, spread, 0.0)), 0.0)
    mixing = (decays * scores[:, None] * jnp.transpose(rate_rows, (1, 2, 0))[:, :, None, :]).astype(jnp.bfloat16)
    local_out = jnp.einsum('gkts,sgkp->tgkp', mixing, input_rows, preferred_element_type=jnp.float32)
    input_float = input_rows.astype(jnp.float32)
    local_out = local_out + skip_rate[None, :, :, None] * input_float
    tail_weight = jnp.exp(cumlog[-1][None] - cumlog) * rate_rows
    weighted = (input_float * tail_weight[..., None]).astype(jnp.bfloat16)
    local_state = jnp.einsum('sgkp,sgn->gkpn', weighted, write_rows, preferred_element_type=jnp.float32)
    return (local_out, cumlog, jnp.exp(cumlog[-1]), local_state)

def carried_term(read_rows, cumlog, state_in):
    inner = jnp.einsum('tgn,gkpn->tgkp', read_rows.astype(jnp.float32), state_in, precision=lax.Precision.HIGHEST)
    return jnp.exp(cumlog)[..., None] * inner

def stretch_full(input_rows, write_rows, read_rows, rate_rows, decay_rate, skip_rate, state_in):
    local_out, cumlog, through, local_state = stretch_parts(input_rows, write_rows, read_rows, rate_rows, decay_rate, skip_rate)
    output = local_out + carried_term(read_rows, cumlog, state_in)
    return (output, through[..., None, None] * state_in + local_state)

def to_sequence(array, stretch_order):
    blocks = array.reshape((PAIRS, 2, STRETCH) + array.shape[1:])
    inverse = jnp.zeros((PAIRS,), jnp.int32).at[stretch_order].set(jnp.arange(PAIRS, dtype=jnp.int32))
    first_half = blocks[inverse, 0]
    second_half = blocks[inverse, 1][::-1]
    return jnp.concatenate([first_half, second_half], axis=0).reshape(array.shape)

def to_layout(array, stretch_order):
    blocks = array.reshape((2 * PAIRS, STRETCH) + array.shape[1:])
    first_half = blocks[stretch_order]
    second_half = blocks[2 * PAIRS - 1 - stretch_order]
    return jnp.stack([first_half, second_half], axis=1).reshape(array.shape)

def attention(query_seq, key_seq, value_seq, grad_seq):
    queries = query_seq.reshape(TOKEN_COUNT, AHEADS, AHD)
    keys_all = key_seq.reshape(TOKEN_COUNT, KVHEADS, AHD)
    values_all = value_seq.reshape(TOKEN_COUNT, KVHEADS, AHD)
    grads_all = grad_seq.reshape(TOKEN_COUNT, AHEADS, AHD)
    per_kv = AHEADS // KVHEADS
    score_scale = AHD ** (-0.5)
    position = jnp.arange(TOKEN_COUNT)
    causal = position[:, None] >= position[None, :]

    def one_head(head_index):
        query_head = queries[:, head_index]
        key_head = keys_all[:, head_index // per_kv]
        value_head = values_all[:, head_index // per_kv]
        grad_head = grads_all[:, head_index]
        scores = jnp.dot(query_head, key_head.T, preferred_element_type=jnp.float32) * score_scale
        scores = jnp.where(causal, scores, -jnp.inf)
        row_peak = lax.optimization_barrier(jnp.max(scores, axis=1, keepdims=True))
        expo = jnp.exp(scores - row_peak)
        row_total = lax.optimization_barrier(jnp.sum(expo, axis=1, keepdims=True))
        output = jnp.dot(expo.astype(jnp.bfloat16), value_head, preferred_element_type=jnp.float32) / row_total
        output_low = lax.optimization_barrier(output.astype(jnp.bfloat16))
        log_total = row_peak + jnp.log(row_total)
        delta_rows = lax.optimization_barrier(jnp.sum(grad_head.astype(jnp.float32) * output_low.astype(jnp.float32), axis=1, keepdims=True))
        probabilities = jnp.exp(scores - log_total)
        prob_grad = jnp.dot(grad_head, value_head.T, preferred_element_type=jnp.float32)
        score_grad = (probabilities * (prob_grad - delta_rows)).astype(jnp.bfloat16)
        query_change = jnp.dot(score_grad, key_head, preferred_element_type=jnp.float32) * score_scale
        return (output_low, query_change.astype(jnp.bfloat16))
    outputs, changes = lax.map(one_head, jnp.arange(AHEADS))
    outputs = jnp.transpose(outputs, (1, 0, 2)).reshape(TOKEN_COUNT, AHEADS * AHD)
    changes = jnp.transpose(changes, (1, 0, 2)).reshape(TOKEN_COUNT, AHEADS * AHD)
    return (outputs, changes)

def mamba_forward(input_seq, write_seq, read_seq, rate_seq, decay_rate, skip_rate, gate_seq, norm_gain):
    per_group = MAMBA_HEAD_HALF // GROUPS
    block_count = 2 * PAIRS
    inputs = input_seq.reshape(block_count, STRETCH, GROUPS, per_group, MDIM)
    writes = write_seq.reshape(block_count, STRETCH, GROUPS, NSTATE)
    reads = read_seq.reshape(block_count, STRETCH, GROUPS, NSTATE)
    rates = rate_seq.reshape(block_count, STRETCH, GROUPS, per_group)

    def advance(state, pieces):
        output, state_next = stretch_full(pieces[0], pieces[1], pieces[2], pieces[3], decay_rate, skip_rate, state)
        return (state_next, output)
    initial = jnp.zeros((GROUPS, per_group, MDIM, NSTATE), jnp.float32)
    final_state, outputs = lax.scan(advance, initial, (inputs, writes, reads, rates))
    mixed = outputs.reshape(TOKEN_COUNT, MAMBA_HEAD_HALF * MDIM)
    gated = mixed * jax.nn.silu(gate_seq.astype(jnp.float32))
    mean_square = lax.optimization_barrier(jnp.mean(gated * gated, axis=-1, keepdims=True))
    return (gated * lax.rsqrt(mean_square + 1e-05) * norm_gain[None]).astype(jnp.bfloat16)

def reference(stretch_order, attn_queries, attn_keys, attn_values, attn_grad, mamba_input, gate_input, state_write, state_read, step_raw, decay_log, skip_gain, norm_gain, mamba_grad):
    attn_seq, query_seq = attention(to_sequence(attn_queries, stretch_order), to_sequence(attn_keys, stretch_order), to_sequence(attn_values, stretch_order), to_sequence(attn_grad, stretch_order))
    per_group = MAMBA_HEAD_HALF // GROUPS
    decay_rate = -jnp.exp(decay_log).reshape(GROUPS, per_group)
    skip_rate = skip_gain.reshape(GROUPS, per_group)
    rate_seq = jax.nn.softplus(to_sequence(step_raw, stretch_order))
    gate_seq = to_sequence(gate_input, stretch_order)

    def forward_of(input_seq, write_seq, read_seq):
        return mamba_forward(input_seq, write_seq, read_seq, rate_seq, decay_rate, skip_rate, gate_seq, norm_gain)
    mamba_seq, pullback = jax.vjp(forward_of, to_sequence(mamba_input, stretch_order), to_sequence(state_write, stretch_order), to_sequence(state_read, stretch_order))
    input_seq_grad, write_seq_grad, read_seq_grad = pullback(to_sequence(mamba_grad, stretch_order))
    return (to_layout(attn_seq, stretch_order), to_layout(query_seq, stretch_order), to_layout(mamba_seq, stretch_order), to_layout(input_seq_grad, stretch_order), to_layout(write_seq_grad, stretch_order), to_layout(read_seq_grad, stretch_order))
```

```python
import jax
import jax.numpy as jnp
from jax import lax
from jax.experimental import pallas as pl
from jax.experimental.pallas import tpu as pltpu
from jax.sharding import PartitionSpec as P

HEAD_CH = 64
NSTATE = 128
AHD = 128
STRETCH = 64
EXTRA = 16
NORM_EPS = 1e-05
NEG_FILL = -1e30
KEY_CHUNK = 512
F32 = jnp.float32
BF16 = jnp.bfloat16
VMEM_BYTES = 48 * 1024 * 1024


def mm(a, b):
    return lax.dot_general(a, b, (((1,), (0,)), ((), ())), preferred_element_type=F32)


def mm_nt(a, b):
    return lax.dot_general(a, b, (((1,), (1,)), ((), ())), preferred_element_type=F32)


def split3(v):
    hi = v.astype(BF16)
    rest = v - hi.astype(F32)
    mid = rest.astype(BF16)
    low = (rest - mid.astype(F32)).astype(BF16)
    return hi, mid, low


def pair_spread(cols, k):
    rows = cols.shape[0]
    lane = lax.broadcasted_iota(jnp.int32, (rows, 128), 1)
    even = jnp.broadcast_to(cols[:, 2 * k : 2 * k + 1], (rows, 128))
    odd = jnp.broadcast_to(cols[:, 2 * k + 1 : 2 * k + 2], (rows, 128))
    return jnp.where(lane < HEAD_CH, even, odd)


def spread(cols, heads):
    return jnp.concatenate([pair_spread(cols, k) for k in range(heads // 2)], axis=1)


def call(fn, outs, args, smem=(), scratch=(), flops=0, nbytes=0):
    specs = [
        pl.BlockSpec(memory_space=pltpu.SMEM if i in smem else pltpu.VMEM)
        for i in range(len(args))
    ]
    return pl.pallas_call(
        fn,
        out_shape=tuple(jax.ShapeDtypeStruct(s, d) for s, d in outs),
        in_specs=specs,
        out_specs=tuple(pl.BlockSpec(memory_space=pltpu.VMEM) for _ in outs),
        scratch_shapes=list(scratch),
        compiler_params=pltpu.CompilerParams(vmem_limit_bytes=VMEM_BYTES),
        cost_estimate=pl.CostEstimate(flops=flops, bytes_accessed=nbytes, transcendentals=0),
    )(*args)


def pack_forward(me, x, w, r, step, group):
    rows, chans = x.shape[0], x.shape[1] // group
    heads = step.shape[1] // group
    width = chans + 2 * NSTATE + 128

    def kernel(me_ref, x_ref, w_ref, r_ref, step_ref, *outs):
        parts = split3(step_ref[...])
        row = lax.broadcasted_iota(jnp.int32, (heads * group, 128), 0)
        col = lax.broadcasted_iota(jnp.int32, (heads * group, 128), 1)
        for m in range(group):
            dest = me_ref[0] ^ m
            out = outs[m]
            out[:, 0:chans] = x_ref[:, pl.ds(pl.multiple_of(dest * chans, 128), chans)]
            at = pl.ds(pl.multiple_of(dest * NSTATE, 128), NSTATE)
            out[:, chans : chans + NSTATE] = w_ref[:, at]
            out[:, chans + NSTATE : chans + 2 * NSTATE] = r_ref[:, at]
            total = jnp.zeros((rows, 128), F32)
            for i in range(3):
                pick = (row - dest * heads == col - i * heads) & (col >= i * heads)
                pick = pick & (col < (i + 1) * heads)
                total = total + mm(parts[i], jnp.where(pick, 1.0, 0.0).astype(BF16))
            out[:, chans + 2 * NSTATE : width] = total.astype(BF16)

    return call(
        kernel, [((rows, width), BF16)] * group, (me, x, w, r, step), smem=(0,), nbytes=2 * x.size * 3
    )


def pack_gate(me, gate, grad, group):
    rows, chans = gate.shape[0], gate.shape[1] // group

    def kernel(me_ref, gate_ref, grad_ref, *outs):
        for m in range(group):
            at = pl.ds(pl.multiple_of((me_ref[0] ^ m) * chans, 128), chans)
            outs[m][:, 0:chans] = gate_ref[:, at]
            outs[m][:, chans : 2 * chans] = grad_ref[:, at]

    return call(
        kernel, [((rows, 2 * chans), BF16)] * group, (me, gate, grad), smem=(0,), nbytes=8 * gate.size
    )


def unpack(me, pieces, widths):
    group, rows = len(pieces), pieces[0].shape[0]

    def kernel(me_ref, *refs):
        outs = refs[group:]
        for m in range(group):
            start = 0
            for out, width in zip(outs, widths):
                at = pl.ds(pl.multiple_of((me_ref[0] ^ m) * width, 128), width)
                out[:, at] = refs[m][:, start : start + width]
                start += width

    return call(
        kernel,
        [((rows, group * width), BF16) for width in widths],
        (me, *pieces),
        smem=(0,),
        nbytes=4 * rows * group * sum(widths),
    )


def row_blocks(group):
    for half in range(2):
        for m in range(group):
            yield half, m, (half * group + m) * STRETCH


def outgoing_state(pieces, info, info_t, small, chans):
    group = len(pieces)
    rows = 2 * group * STRETCH
    heads = chans // HEAD_CH

    def kernel(*refs):
        ins = refs[:group]
        info_ref, info_t_ref, small_ref = refs[group : group + 3]
        msg, x_out, w_out, r_out, cum_out, rate_out, tail_out, step_buf = refs[group + 3 :]
        for half, m, at in row_blocks(group):
            src = slice(half * STRETCH, (half + 1) * STRETCH)
            x_out[at : at + STRETCH, :] = ins[m][src, 0:chans]
            w_out[at : at + STRETCH, :] = ins[m][src, chans : chans + NSTATE]
            r_out[at : at + STRETCH, :] = ins[m][src, chans + NSTATE : chans + 2 * NSTATE]
            step_buf[at : at + STRETCH, :] = ins[m][src, chans + 2 * NSTATE :]
        row = lax.broadcasted_iota(jnp.int32, (128, 128), 0)
        col = lax.broadcasted_iota(jnp.int32, (128, 128), 1)
        pick = ((row == col) | (row == col + heads) | (row == col + 2 * heads)) & (col < heads)
        step = mm(step_buf[...], jnp.where(pick, 1.0, 0.0).astype(BF16))
        rate = jnp.maximum(step, 0.0) + jnp.log1p(jnp.exp(-jnp.abs(step)))
        rate_out[...] = rate
        amount = rate * small_ref[0:1, :]
        pos_row = info_t_ref[0:1, :]
        same = (pos_row <= info_ref[:, 0:1]) & (pos_row >= info_ref[:, 1:2])
        same = jnp.where(same, 1.0, 0.0).astype(BF16)
        hi, mid, low = split3(amount)
        cum = mm(same, hi) + mm(same, mid) + mm(same, low)
        cum_out[...] = cum
        totals = [
            jnp.sum(amount * info_ref[:, 2 + q : 3 + q], axis=0, keepdims=True) for q in range(2)
        ]
        tail = jnp.zeros_like(cum)
        for q in range(2):
            tail = tail + info_ref[:, 2 + q : 3 + q] * jnp.exp(jnp.minimum(totals[q] - cum, 0.0))
        tail_out[...] = tail
        scale = rate * tail
        w_t = w_out[...].astype(F32).T
        w_q = [(w_t * info_t_ref[2 + q : 3 + q, :]).astype(BF16) for q in range(2)]
        sub = lax.broadcasted_iota(jnp.int32, (EXTRA, 128), 0)
        for k in range(heads // 2):
            lanes = slice(128 * k, 128 * (k + 1))
            xw = (x_out[:, lanes].astype(F32) * pair_spread(scale, k)).astype(BF16)
            for q in range(2):
                msg[q, 0:NSTATE, lanes] = mm(w_q[q], xw).astype(BF16)
                wide = pair_spread(jnp.broadcast_to(totals[q], (EXTRA, 128)), k)
                hi, mid, low = split3(wide)
                hi, mid, low = hi.astype(F32), mid.astype(F32), low.astype(F32)
                msg[q, NSTATE:, lanes] = jnp.where(
                    sub == 0, hi, jnp.where(sub == 1, mid, low)
                ).astype(BF16)

    return call(
        kernel,
        [
            ((2, NSTATE + EXTRA, chans), BF16),
            ((rows, chans), BF16),
            ((rows, NSTATE), BF16),
            ((rows, NSTATE), BF16),
            ((rows, 128), F32),
            ((rows, 128), F32),
            ((rows, 128), F32),
        ],
        (*pieces, info, info_t, small),
        scratch=[pltpu.VMEM((rows, 128), BF16)],
        flops=4 * rows * NSTATE * chans,
        nbytes=6 * rows * chans,
    )


def intra_forward(x, w, r, cum, rate, info, info_t, chan):
    rows, chans = x.shape
    heads = chans // HEAD_CH
    mid = rows // 2

    def kernel(x_ref, w_ref, r_ref, cum_ref, rate_ref, info_ref, info_t_ref, chan_ref, y_ref, gm):
        cum_t = cum_ref[...].T
        lane = lax.broadcasted_iota(jnp.int32, (mid, 128), 1)
        spans = ((0, mid, mid), (mid, mid, rows))
        for start, count, depth in spans:
            at = slice(start, start + count)
            pos_row = info_t_ref[0:1, 0:depth]
            same = (pos_row <= info_ref[at, 0:1]) & (pos_row >= info_ref[at, 1:2])
            gm[at, 0:depth] = jnp.where(same, mm_nt(r_ref[at, :], w_ref[0:depth, :]), 0.0)
        for k in range(heads // 2):
            lanes = slice(128 * k, 128 * (k + 1))
            xf = x_ref[:, lanes].astype(F32)
            xr = (xf * pair_spread(rate_ref[...], k)).astype(BF16)
            for start, count, depth in spans:
                at = slice(start, start + count)
                both = []
                for h in (2 * k, 2 * k + 1):
                    gap = cum_ref[at, h : h + 1] - cum_t[h : h + 1, 0:depth]
                    mix = (jnp.exp(jnp.minimum(gap, 0.0)) * gm[at, 0:depth]).astype(BF16)
                    both.append(mm(mix, xr[0:depth]))
                y_ref[at, lanes] = jnp.where(lane < HEAD_CH, both[0], both[1]) + (
                    chan_ref[0:1, lanes] * xf[at]
                )

    return call(
        kernel,
        [((rows, chans), F32)],
        (x, w, r, cum, rate, info, info_t, chan),
        scratch=[pltpu.VMEM((rows, rows), F32)],
        flops=4 * rows * rows * chans,
        nbytes=8 * rows * chans,
    )[0]


def gather_states(refs, weight, store):
    for q in range(2):
        total = None
        index = 0
        for ref in refs:
            for k in range(ref.shape[0]):
                for c in range(2):
                    term = weight(q, index) * ref[k, c, 0:NSTATE, :].astype(F32)
                    total = term if total is None else total + term
                    index += 1
        store(q, total)


def mixed_rows(msgs, y, r, cum, gates, info, chan, before_in, ends, enter_mask, own_mask, own_end):
    rows, chans = y.shape
    heads = chans // HEAD_CH
    group = len(gates)
    n_msg = len(msgs)
    classes = ends.shape[0]

    def kernel(*refs):
        msg_refs = refs[:n_msg]
        gate_refs = refs[n_msg : n_msg + group]
        (
            y_ref, r_ref, cum_ref, info_ref, chan_ref,
            before_ref, ends_ref, own_ref, own_end_ref, mask_ref,
            gated_ref, sums_ref, state_ref, enter_ref, leave_ref,
            tot, inner, cols,
        ) = refs[n_msg + group :]
        index = 0
        for ref in msg_refs:
            for k in range(ref.shape[0]):
                for c in range(2):
                    part = ref[k, c, NSTATE : NSTATE + EXTRA, :].astype(F32)
                    tot[index : index + 1, :] = part[0:1] + part[1:2] + part[2:3]
                    index += 1
        exact = lax.Precision.HIGHEST
        totals = tot[...]
        enter_ref[...] = jnp.dot(before_ref[...], totals, precision=exact, preferred_element_type=F32)
        leave_all = jnp.dot(ends_ref[...], totals, precision=exact, preferred_element_type=F32)
        own_in = jnp.dot(own_ref[...], totals, precision=exact, preferred_element_type=F32)
        leave_ref[...] = jnp.dot(
            own_end_ref[...], totals, precision=exact, preferred_element_type=F32
        )

        def weight(q, c):
            gap = own_in[q : q + 1] - leave_all[c : c + 1]
            return jnp.exp(jnp.minimum(gap, 0.0)) * mask_ref[q, c]

        def store(q, value):
            state_ref[q * NSTATE : (q + 1) * NSTATE, :] = value.astype(BF16)

        gather_states(msg_refs, weight, store)
        reads = r_ref[...].astype(F32)
        both = jnp.concatenate(
            [(reads * info_ref[:, 4:5]).astype(BF16), (reads * info_ref[:, 5:6]).astype(BF16)], axis=1
        )
        inner[...] = mm(both, state_ref[...])
        lane = lax.broadcasted_iota(jnp.int32, (STRETCH, 128), 1)
        for half, m, at in row_blocks(group):
            here = slice(at, at + STRETCH)
            src = slice(half * STRETCH, (half + 1) * STRETCH)
            mixed = y_ref[here, :] + spread(jnp.exp(cum_ref[here, :]), heads) * inner[here, :]
            gate = gate_refs[m][src, 0:chans].astype(F32)
            gated = mixed * (gate / (1.0 + jnp.exp(-gate)))
            gated_ref[here, :] = gated
            grad = gate_refs[m][src, chans : 2 * chans].astype(F32) * chan_ref[1:2, :]
            square = jnp.sum(gated * gated, axis=1, keepdims=True)
            cross = jnp.sum(grad * gated, axis=1, keepdims=True)
            cols[here, :] = jnp.where(lane == 0, square, jnp.where(lane == 1, cross, 0.0))
        sums_ref[...] = cols[...].T[0:8, :]

    args = (
        *msgs, *gates, y, r, cum, info, chan, before_in, ends, own_mask, own_end, enter_mask
    )
    return call(
        kernel,
        [
            ((rows, chans), F32),
            ((8, rows), F32),
            ((2 * NSTATE, chans), BF16),
            ((classes, chans), F32),
            ((8, chans), F32),
        ],
        args,
        smem=(len(args) - 1,),
        scratch=[
            pltpu.VMEM((classes, chans), F32),
            pltpu.VMEM((rows, chans), F32),
            pltpu.VMEM((rows, 128), F32),
        ],
        flops=4 * rows * 2 * NSTATE * chans,
        nbytes=16 * rows * chans,
    )


def mixed_cotangent(sums, gated, gates, r, cum, info_t, chan, total_chans):
    rows, chans = gated.shape
    heads = chans // HEAD_CH
    group = len(gates)

    def kernel(*refs):
        gate_refs = refs[:group]
        sums_refs, refs = refs[group : 2 * group], refs[2 * group :]
        gated_ref, r_ref, cum_ref, info_t_ref, chan_ref, touch_ref, dmix_ref, lift_ref = refs[:8]
        outs = refs[8 : 8 + group]
        cols = refs[8 + group]
        parts = [ref[...] for ref in sums_refs]
        both = jnp.concatenate(parts + [jnp.zeros((128 - 8 * group, rows), F32)], axis=0)
        cols[...] = both.T
        for half, m, at in row_blocks(group):
            here = slice(at, at + STRETCH)
            src = slice(half * STRETCH, (half + 1) * STRETCH)
            square = cross = 0.0
            for peer in range(group):
                start = (half * group + (m ^ peer)) * STRETCH
                there = slice(start, start + STRETCH)
                square = square + cols[there, 8 * peer : 8 * peer + 1]
                cross = cross + cols[there, 8 * peer + 1 : 8 * peer + 2]
            inv = lax.rsqrt(square / total_chans + NORM_EPS)
            pull = inv * inv * inv * (cross / total_chans)
            gated = gated_ref[here, :]
            gain = chan_ref[1:2, :]
            outs[m][src, :] = (gated * inv * gain).astype(BF16)
            gate = gate_refs[m][src, 0:chans].astype(F32)
            grad = gate_refs[m][src, chans : 2 * chans].astype(F32) * gain
            dmix = (inv * grad - gated * pull) * (gate / (1.0 + jnp.exp(-gate)))
            dmix_ref[here, :] = dmix
            lift_ref[here, :] = (dmix * spread(jnp.exp(cum_ref[here, :]), heads)).astype(BF16)
        r_t = r_ref[...].astype(F32).T
        for q in range(2):
            left = (r_t * info_t_ref[4 + q : 5 + q, :]).astype(BF16)
            touch_ref[q] = mm(left, lift_ref[...]).astype(BF16)

    return call(
        kernel,
        [
            ((2, NSTATE, chans), BF16),
            ((rows, chans), F32),
            ((rows, chans), BF16),
            *[((2 * STRETCH, chans), BF16)] * group,
        ],
        (*gates, *sums, gated, r, cum, info_t, chan),
        scratch=[pltpu.VMEM((rows, 128), F32)],
        flops=4 * rows * NSTATE * chans,
        nbytes=16 * rows * chans,
    )


def intra_backward(x, w, r, cum, rate, dmix, lift, state, info, info_t):
    rows, chans = x.shape
    heads = chans // HEAD_CH
    mid = rows // 2

    def kernel(
        x_ref, w_ref, r_ref, cum_ref, rate_ref, dmix_ref, lift_ref, state_ref, info_ref, info_t_ref,
        dx_ref, dw_ref, dr_ref, gm, dgm,
    ):
        cum_t = cum_ref[...].T
        lane = lax.broadcasted_iota(jnp.int32, (rows, 128), 1)
        lane_mid = lax.broadcasted_iota(jnp.int32, (mid, 128), 1)
        spans = ((0, 0), (mid, mid))

        def same_of(start, later):
            pos = info_ref[start : start + mid, 0:1]
            return (pos <= info_t_ref[0:1, later:]) & (pos >= info_t_ref[1:2, later:])

        for start, later in spans:
            at = slice(start, start + mid)
            product = mm_nt(w_ref[at, :], r_ref[later:, :])
            gm[at, later:] = jnp.where(same_of(start, later), product, 0.0)
        for k in range(heads // 2):
            lanes = slice(128 * k, 128 * (k + 1))
            xr = x_ref[:, lanes].astype(F32) * pair_spread(rate_ref[...], k)
            parts = (
                jnp.where(lane < HEAD_CH, xr, 0.0).astype(BF16),
                jnp.where(lane < HEAD_CH, 0.0, xr).astype(BF16),
            )
            grads = dmix_ref[:, lanes].astype(BF16)
            for start, later in spans:
                at = slice(start, start + mid)
                both = []
                for i in range(2):
                    h = 2 * k + i
                    gap = cum_t[h : h + 1, later:] - cum_ref[at, h : h + 1]
                    fade = jnp.exp(jnp.minimum(gap, 0.0))
                    mix = (fade * gm[at, later:]).astype(BF16)
                    both.append(mm(mix, grads[later:]))
                    change = fade * mm_nt(parts[i][at], grads[later:])
                    if h == 0:
                        dgm[at, later:] = change
                    else:
                        dgm[at, later:] += change
                dx_ref[at, lanes] = jnp.where(lane_mid < HEAD_CH, both[0], both[1])
        carried = mm_nt(lift_ref[...], state_ref[0:NSTATE, :]) * info_ref[:, 4:5]
        carried = carried + mm_nt(lift_ref[...], state_ref[NSTATE:, :]) * info_ref[:, 5:6]
        dr_ref[...] = carried
        for start, later in spans:
            at = slice(start, start + mid)
            change = jnp.where(same_of(start, later), dgm[at, later:], 0.0)
            dw_ref[at, :] = mm(change.astype(BF16), r_ref[later:, :])
            dr_ref[later:, :] += mm(change.T.astype(BF16), w_ref[at, :])

    return call(
        kernel,
        [((rows, chans), F32), ((rows, NSTATE), F32), ((rows, NSTATE), F32)],
        (x, w, r, cum, rate, dmix, lift, state, info, info_t),
        scratch=[pltpu.VMEM((rows, rows), F32), pltpu.VMEM((rows, rows), F32)],
        flops=8 * rows * rows * chans,
        nbytes=16 * rows * chans,
    )


def final_grads(msgs, x, w, rate, tail, dx, dw, dr, dmix, info, chan, enter, leave, leave_mask):
    rows, chans = x.shape
    heads = chans // HEAD_CH
    group = rows // (2 * STRETCH)
    n_msg = len(msgs)
    width = chans + 2 * NSTATE

    def kernel(*refs):
        msg_refs = refs[:n_msg]
        (
            x_ref, w_ref, rate_ref, tail_ref, dx_ref, dw_ref, dr_ref, dmix_ref, info_ref, chan_ref,
            enter_ref, leave_ref, mask_ref,
        ) = refs[n_msg : n_msg + 13]
        outs = refs[n_msg + 13 : n_msg + 13 + group]
        after, inner, xw = refs[n_msg + 13 + group :]

        def weight(q, c):
            gap = enter_ref[c : c + 1, :] - leave_ref[q : q + 1, :]
            return jnp.exp(jnp.minimum(gap, 0.0)) * mask_ref[q, c]

        def store(q, value):
            after[q * NSTATE : (q + 1) * NSTATE, :] = value.astype(BF16)

        gather_states(msg_refs, weight, store)
        writes = w_ref[...].astype(F32)
        both = jnp.concatenate(
            [(writes * info_ref[:, 2:3]).astype(BF16), (writes * info_ref[:, 3:4]).astype(BF16)],
            axis=1,
        )
        inner[...] = mm(both, after[...])
        for half, m, at in row_blocks(group):
            here = slice(at, at + STRETCH)
            dst = slice(half * STRETCH, (half + 1) * STRETCH)
            rates = spread(rate_ref[here, :], heads)
            tails = spread(tail_ref[here, :], heads)
            xw[here, :] = (x_ref[here, :].astype(F32) * (rates * tails)).astype(BF16)
            change = rates * (dx_ref[here, :] + tails * inner[here, :])
            change = change + chan_ref[0:1, :] * dmix_ref[here, :]
            outs[m][dst, 0:chans] = change.astype(BF16)
            outs[m][dst, chans + NSTATE :] = dr_ref[here, :].astype(BF16)
        change = dw_ref[...] + mm_nt(xw[...], after[0:NSTATE, :]) * info_ref[:, 2:3]
        change = change + mm_nt(xw[...], after[NSTATE:, :]) * info_ref[:, 3:4]
        for half, m, at in row_blocks(group):
            dst = slice(half * STRETCH, (half + 1) * STRETCH)
            outs[m][dst, chans : chans + NSTATE] = change[at : at + STRETCH].astype(BF16)

    args = (
        *msgs, x, w, rate, tail, dx, dw, dr, dmix, info, chan, enter, leave, leave_mask
    )
    return call(
        kernel,
        [((2 * STRETCH, width), BF16)] * group,
        args,
        smem=(len(args) - 1,),
        scratch=[
            pltpu.VMEM((2 * NSTATE, chans), BF16),
            pltpu.VMEM((rows, chans), F32),
            pltpu.VMEM((rows, chans), BF16),
        ],
        flops=8 * rows * NSTATE * chans,
        nbytes=16 * rows * chans,
    )


def attention(blocks, own_blocks, pieces, queries, grads, kv_heads):
    rows = queries.shape[0]
    per_kv = queries.shape[1] // AHD // kv_heads
    group, units = len(pieces), pieces[0].shape[0]
    tokens = group * units * rows
    half_width = kv_heads * AHD
    scale = AHD ** (-0.5)
    chunk = min(KEY_CHUNK, tokens)
    tall = per_kv * STRETCH

    def kernel(*refs):
        blocks_ref, own_ref = refs[:2]
        piece_refs = refs[2 : 2 + group]
        q_ref, g_ref, out_ref, dq_ref, kv, scores = refs[2 + group :]
        for m in range(group):
            for u in range(units):
                for half in range(2):
                    at = pl.ds(pl.multiple_of(blocks_ref[half, m * units + u] * STRETCH, 64), STRETCH)
                    kv[at, :] = piece_refs[m][u, half * STRETCH : (half + 1) * STRETCH, :]
        offset = lax.broadcasted_iota(jnp.int32, (tall, chunk), 0) % STRETCH
        column = lax.broadcasted_iota(jnp.int32, (tall, chunk), 1)
        for half in range(2):
            block = own_ref[half]
            src = slice(half * STRETCH, (half + 1) * STRETCH)
            steps = (block * STRETCH) // chunk + 1
            reach = offset + block * STRETCH
            for g in range(kv_heads):
                k_at = slice(g * AHD, (g + 1) * AHD)
                v_at = slice(half_width + g * AHD, half_width + (g + 1) * AHD)
                heads = [slice((g * per_kv + i) * AHD, (g * per_kv + i + 1) * AHD) for i in range(per_kv)]
                query = jnp.concatenate([q_ref[src, at] for at in heads], axis=0)
                grad = jnp.concatenate([g_ref[src, at] for at in heads], axis=0)

                def keys_of(c):
                    return pl.ds(pl.multiple_of(c * chunk, chunk), chunk)

                def first(c, peak):
                    value = mm_nt(query, kv[keys_of(c), k_at]) * scale
                    value = jnp.where(column + c * chunk <= reach, value, NEG_FILL)
                    scores[c] = value
                    return jnp.maximum(peak, jnp.max(value, axis=1, keepdims=True))

                peak = lax.fori_loop(0, steps, first, jnp.full((tall, 1), NEG_FILL, F32))

                def second(c, carry):
                    total, out = carry
                    value = jnp.exp(scores[c] - peak)
                    scores[c] = value
                    out = out + mm(value.astype(BF16), kv[keys_of(c), v_at])
                    return total + jnp.sum(value, axis=1, keepdims=True), out

                total, out = lax.fori_loop(
                    0, steps, second, (jnp.zeros((tall, 1), F32), jnp.zeros((tall, AHD), F32))
                )
                out = (out / total).astype(BF16)
                delta = jnp.sum(grad.astype(F32) * out.astype(F32), axis=1, keepdims=True)

                def third(c, acc):
                    slope = mm_nt(grad, kv[keys_of(c), v_at]) - delta
                    change = (scores[c] * slope).astype(BF16)
                    return acc + mm(change, kv[keys_of(c), k_at])

                acc = lax.fori_loop(0, steps, third, jnp.zeros((tall, AHD), F32))
                acc = (acc * (scale / total)).astype(BF16)
                for i, at in enumerate(heads):
                    out_ref[src, at] = out[i * STRETCH : (i + 1) * STRETCH]
                    dq_ref[src, at] = acc[i * STRETCH : (i + 1) * STRETCH]

    return call(
        kernel,
        [(queries.shape, BF16), (queries.shape, BF16)],
        (blocks, own_blocks, *pieces, queries, grads),
        smem=(0, 1),
        scratch=[
            pltpu.VMEM((tokens, 2 * half_width), BF16),
            pltpu.VMEM((tokens // chunk, tall, chunk), F32),
        ],
        flops=10 * queries.size * tokens,
        nbytes=4 * tokens * half_width,
    )


def body(
    stretch_order,
    attn_queries,
    attn_keys,
    attn_values,
    attn_grad,
    mamba_input,
    gate_input,
    state_write,
    state_read,
    step_raw,
    decay_log,
    skip_gain,
    norm_gain,
    mamba_grad,
):
    ctx_count = lax.axis_size("ctx")
    tp_count = lax.axis_size("tp")
    group = state_write.shape[1] // NSTATE
    units = ctx_count // group
    by_permute = units <= 4
    my_index = lax.axis_index("ctx")
    my_unit, my_place = my_index // group, my_index % group
    me = my_place.astype(jnp.int32).reshape(1)
    chans = mamba_input.shape[1] // group
    heads = chans // HEAD_CH
    kv_heads = attn_keys.shape[1] // AHD
    turn = stretch_order[0]
    last = 2 * ctx_count

    def in_plane(values):
        moved = [values[0]]
        for m in range(1, group):
            pairs = [(i, (i // group) * group + ((i % group) ^ m)) for i in range(ctx_count)]
            moved.append(lax.ppermute(values[m], "ctx", pairs))
        return moved

    def across(value):
        moved = [value]
        for m in range(1, units):
            pairs = [(i, ((i // group) ^ m) * group + i % group) for i in range(ctx_count)]
            moved.append(lax.ppermute(value, "ctx", pairs))
        return moved

    def all_units(value):
        if by_permute:
            return [part[None] for part in across(value)]
        if group == 1:
            return [lax.all_gather(value, "ctx", axis=0)]
        sets = [[u * group + j for u in range(units)] for j in range(group)]
        return [lax.all_gather(value, "ctx", axis=0, axis_index_groups=sets)]

    own_kv = jnp.concatenate([attn_keys, attn_values], axis=1)
    kv_units = all_units(own_kv)

    packed = pack_forward(me, mamba_input, state_write, state_read, step_raw, group)
    forward_pieces = in_plane(packed)
    gates = in_plane(pack_gate(me, gate_input, mamba_grad, group))

    unit_ids = jnp.arange(units, dtype=jnp.int32)
    if by_permute:
        unit_ids = unit_ids ^ my_unit
    place_ids = jnp.arange(group, dtype=jnp.int32) ^ my_place

    def class_bounds(unit):
        first = (unit * group + turn) % ctx_count
        wraps = first + group > ctx_count
        extra = first + group - ctx_count
        out_start = (jnp.where(wraps, 0, first), jnp.where(wraps, first, last - first - group))
        out_end = (jnp.where(wraps, extra, first + group), last - first)
        in_start = (first, jnp.where(wraps, last - extra, last - first - group))
        in_end = (
            jnp.where(wraps, last - first, first + group),
            jnp.where(wraps, last, last - first),
        )
        return out_start, out_end, in_start, in_end

    out_start, out_end, in_start, in_end = class_bounds(my_unit)
    _, all_out_end, all_in_start, _ = class_bounds(unit_ids)
    all_out_end = jnp.stack(all_out_end, axis=1).reshape(-1)
    all_in_start = jnp.stack(all_in_start, axis=1).reshape(-1)
    own_out_end = jnp.stack(out_end)
    own_in_start = jnp.stack(in_start)
    enter_mask = (all_out_end[None, :] <= own_in_start[:, None]).astype(F32)
    leave_mask = (own_out_end[:, None] <= all_in_start[None, :]).astype(F32)
    own_end = (all_out_end[None, :] <= own_out_end[:, None]).astype(F32)
    before_in = (all_out_end[None, :] <= all_in_start[:, None]).astype(F32)
    ends = (all_out_end[None, :] <= all_out_end[:, None]).astype(F32)
    own_mask = jnp.concatenate([enter_mask, jnp.zeros((6, 2 * units), F32)], axis=0)
    own_end = jnp.concatenate([own_end, jnp.zeros((6, 2 * units), F32)], axis=0)

    def info_of(row):
        half, place, offset = row // (group * STRETCH), (row // STRETCH) % group, row % STRETCH
        pair = (my_unit * group + (place ^ my_place) + turn) % ctx_count
        block = jnp.where(half == 0, pair, last - 1 - pair)

        def within(start, end):
            return ((block >= start) & (block < end)).astype(F32)

        low = jnp.where(
            within(in_start[1], in_end[1]) > 0,
            in_start[1],
            jnp.where(within(in_start[0], in_end[0]) > 0, in_start[0], out_start[0]),
        )
        return [
            (block * STRETCH + offset).astype(F32),
            (low * STRETCH).astype(F32),
            within(out_start[0], out_end[0]),
            within(out_start[1], out_end[1]),
            within(in_start[0], in_end[0]),
            within(in_start[1], in_end[1]),
        ]

    rows = 2 * group * STRETCH
    cols = info_of(lax.broadcasted_iota(jnp.int32, (rows, 8), 0))
    pick = lax.broadcasted_iota(jnp.int32, (rows, 8), 1)
    info = sum(jnp.where(pick == i, c, 0.0) for i, c in enumerate(cols))
    cols = info_of(lax.broadcasted_iota(jnp.int32, (8, rows), 1))
    pick = lax.broadcasted_iota(jnp.int32, (8, rows), 0)
    info_t = sum(jnp.where(pick == i, c, 0.0) for i, c in enumerate(cols))

    decay = -jnp.exp(lax.dynamic_slice(decay_log, (my_place * heads,), (heads,)))
    small = jnp.pad(decay[None], ((0, 7), (0, 128 - heads)))
    skip = jnp.repeat(lax.dynamic_slice(skip_gain, (my_place * heads,), (heads,)), HEAD_CH)
    gain = lax.dynamic_slice(norm_gain, (my_place * chans,), (chans,))
    chan = jnp.pad(jnp.stack([skip, gain]), ((0, 6), (0, 0)))

    msg, x, w, r, cum, rate, tail = outgoing_state(forward_pieces, info, info_t, small, chans)
    msgs = all_units(msg)

    kv_all = kv_units[0] if len(kv_units) == 1 else jnp.concatenate(kv_units, axis=0)
    kv_pieces = in_plane([kv_all] * group)

    y = intra_forward(x, w, r, cum, rate, info, info_t, chan)
    gated, sums, state, enter, leave = mixed_rows(
        msgs, y, r, cum, gates, info, chan, before_in, ends, enter_mask, own_mask, own_end
    )
    if tp_count == 2:
        sums = sums + lax.ppermute(sums, "tp", [(0, 1), (1, 0)])
    else:
        sums = lax.psum(sums, "tp")
    sums = in_plane([sums] * group)
    touch, dmix, lift, *out_pieces = mixed_cotangent(
        sums, gated, gates, r, cum, info_t, chan, float(mamba_input.shape[1] * tp_count)
    )
    touches = all_units(touch)
    (mamba_output,) = unpack(me, in_plane(out_pieces), (chans,))
    dx, dw, dr = intra_backward(x, w, r, cum, rate, dmix, lift, state, info, info_t)

    pair_table = (unit_ids[None, :] * group + place_ids[:, None] + turn) % ctx_count
    pair_table = pair_table.reshape(1, -1)
    blocks = jnp.concatenate([pair_table, last - 1 - pair_table], axis=0)
    attn_output, query_grad = attention(
        blocks, blocks[:, 0] if by_permute else jnp.stack(
            [(my_index + turn) % ctx_count, last - 1 - (my_index + turn) % ctx_count]
        ),
        kv_pieces, attn_queries, attn_grad, kv_heads,
    )

    finals = final_grads(
        touches, x, w, rate, tail, dx, dw, dr, dmix, info, chan, enter, leave, leave_mask
    )
    input_grad, write_grad, read_grad = unpack(me, in_plane(finals), (chans, NSTATE, NSTATE))
    return (attn_output, query_grad, mamba_output, input_grad, write_grad, read_grad)


def solution(mesh):
    wide, flat = P("ctx", "tp"), P("tp")
    return jax.shard_map(
        body,
        mesh=mesh,
        in_specs=(P(),) + (wide,) * 9 + (flat,) * 3 + (wide,),
        out_specs=(wide,) * 6,
        check_vma=False,
    )
```

```python
import jax
import jax.numpy as jnp
from jax import lax
from jax.experimental import pallas as pl
from jax.experimental.pallas import tpu as pltpu
from jax.sharding import PartitionSpec as P

HEAD_CH = 64
NSTATE = 128
AHD = 128
STRETCH = 64
EXTRA = 16
NORM_EPS = 1e-05
NEG_FILL = -1e30
KEY_CHUNK = 512
LOG2_E = 1.4426950408889634
F32 = jnp.float32
BF16 = jnp.bfloat16
MIB = 1024 * 1024


def after(value, event):
    return lax.optimization_barrier((value, event))[0]


def mm(a, b):
    return lax.dot_general(a, b, (((1,), (0,)), ((), ())), preferred_element_type=F32)


def mm_nt(a, b):
    return lax.dot_general(a, b, (((1,), (1,)), ((), ())), preferred_element_type=F32)


def split3(v):
    hi = v.astype(BF16)
    rest = v - hi.astype(F32)
    mid = rest.astype(BF16)
    low = (rest - mid.astype(F32)).astype(BF16)
    return hi, mid, low


def pair_spread(cols, k):
    rows = cols.shape[0]
    lane = lax.broadcasted_iota(jnp.int32, (rows, 128), 1)
    even = jnp.broadcast_to(cols[:, 2 * k : 2 * k + 1], (rows, 128))
    odd = jnp.broadcast_to(cols[:, 2 * k + 1 : 2 * k + 2], (rows, 128))
    return jnp.where(lane < HEAD_CH, even, odd)


def spread(cols, heads):
    return jnp.concatenate([pair_spread(cols, k) for k in range(heads // 2)], axis=1)


def call(fn, outs, args, smem=(), scratch=(), flops=0, nbytes=0, mib=12):
    specs = [
        pl.BlockSpec(memory_space=pltpu.SMEM if i in smem else pltpu.VMEM)
        for i in range(len(args))
    ]
    return pl.pallas_call(
        fn,
        out_shape=tuple(jax.ShapeDtypeStruct(s, d) for s, d in outs),
        in_specs=specs,
        out_specs=tuple(pl.BlockSpec(memory_space=pltpu.VMEM) for _ in outs),
        scratch_shapes=list(scratch),
        compiler_params=pltpu.CompilerParams(vmem_limit_bytes=mib * MIB),
        cost_estimate=pl.CostEstimate(flops=flops // 1000, bytes_accessed=nbytes // 1000, transcendentals=0),
    )(*args)


def pack_forward(x, w, r, step, gate, grad, keys, values, group):
    rows, chans = x.shape[0], x.shape[1] // group
    heads = step.shape[1] // group
    width = chans + 2 * NSTATE + 128
    kv_width = keys.shape[1]

    wide = [(0, chans), (1, NSTATE), (2, NSTATE), (None, 128), (3, chans), (4, chans)]
    sources = (x, w, r, gate, grad, keys, values)
    n_in = len(sources)
    n_out = 2 + group * len(wide)

    def kernel(step_ref, *refs):
        ins, kv_ref, out, gate_out = refs[:n_in], *refs[n_in : n_in + 3]
        held = refs[n_in + 3 : -3]
        step_buf, in_sems, out_sems = refs[-3:]
        loads = [pltpu.make_async_copy(ins[i], held[i], in_sems.at[i]) for i in range(n_in)]
        for i in (5, 6, 0, 1, 2, 3, 4):
            loads[i].start()
        parts = split3(step_ref[...])
        row = lax.broadcasted_iota(jnp.int32, (heads * group, 128), 0)
        col = lax.broadcasted_iota(jnp.int32, (heads * group, 128), 1)
        for m in range(group):
            total = jnp.zeros((rows, 128), F32)
            for i in range(3):
                pick = (row - m * heads == col - i * heads) & (col >= i * heads)
                pick = pick & (col < (i + 1) * heads)
                total = total + mm(parts[i], jnp.where(pick, 1.0, 0.0).astype(BF16))
            step_buf[m] = total.astype(BF16)
        copies = []

        def send(src, dst):
            copy = pltpu.make_async_copy(src, dst, out_sems.at[len(copies)])
            copy.start()
            copies.append(copy)

        loads[5].wait()
        send(held[5], kv_ref.at[:, 0:kv_width])
        loads[6].wait()
        send(held[6], kv_ref.at[:, kv_width : 2 * kv_width])
        start = 0
        for source, count in wide:
            if source is not None:
                loads[source].wait()
            for m in range(group):
                at = slice(m * count, (m + 1) * count)
                if start >= width:
                    dst = gate_out.at[m, :, start - width : start - width + count]
                else:
                    dst = out.at[m, :, start : start + count]
                send(step_buf.at[m] if source is None else held[source].at[:, at], dst)
            start += count
        for copy in copies:
            copy.wait()

    return move(
        kernel,
        [((rows, 2 * kv_width), BF16)]
        + [((group, rows, width), BF16), ((group, rows, 2 * chans), BF16)],
        (step, *sources),
        (pltpu.VMEM,),
        [pltpu.VMEM(source.shape, BF16) for source in sources]
        + [
            pltpu.VMEM((group, rows, 128), BF16),
            pltpu.SemaphoreType.DMA((n_in,)),
            pltpu.SemaphoreType.DMA((n_out,)),
        ],
        mib=60,
    )


def move(fn, outs, args, spaces, scratch, mib=8):
    spaces = tuple(spaces) + (pl.ANY,) * (len(args) - len(spaces))
    return pl.pallas_call(
        fn,
        out_shape=tuple(jax.ShapeDtypeStruct(s, d) for s, d in outs),
        in_specs=[pl.BlockSpec(memory_space=space) for space in spaces],
        out_specs=tuple(pl.BlockSpec(memory_space=pl.ANY) for _ in outs),
        scratch_shapes=scratch,
        compiler_params=pltpu.CompilerParams(vmem_limit_bytes=mib * MIB),
        cost_estimate=pl.CostEstimate(flops=0, bytes_accessed=1024, transcendentals=0),
    )(*args)


def stack_parts(parts):
    count = len(parts)

    def kernel(*refs):
        for i in range(count):
            refs[count][i] = refs[i][0]

    shape = (count,) + parts[0].shape[1:]
    return call(kernel, [(shape, BF16)], parts, nbytes=4 * count * parts[0].size)[0]


def unpack(me, pieces, widths):
    group, rows = len(pieces), pieces[0].shape[0]

    def kernel(me_ref, *refs):
        outs = refs[group:]
        for m in range(group):
            start = 0
            for out, width in zip(outs, widths):
                at = pl.ds(pl.multiple_of((me_ref[0] ^ m) * width, 128), width)
                out[:, at] = refs[m][:, start : start + width]
                start += width

    return call(
        kernel,
        [((rows, group * width), BF16) for width in widths],
        (me, *pieces),
        smem=(0,),
        nbytes=4 * rows * group * sum(widths),
    )


def row_blocks(group):
    for half in range(2):
        for m in range(group):
            yield half, m, (half * group + m) * STRETCH


def outgoing_state(me, pieces, info, info_t, small, chans):
    group = pieces.shape[0]
    rows = 2 * group * STRETCH
    heads = chans // HEAD_CH

    def kernel(*refs):
        me_ref, ins, info_ref, info_t_ref, small_ref = refs[:5]
        msg, x_out, w_out, r_out, cum_out, rate_out, tail_out, step_buf = refs[5:]
        for half, m, at in row_blocks(group):
            src = slice(half * STRETCH, (half + 1) * STRETCH)
            x_out[at : at + STRETCH, :] = ins[me_ref[0] ^ m, src, 0:chans]
            w_out[at : at + STRETCH, :] = ins[me_ref[0] ^ m, src, chans : chans + NSTATE]
            r_out[at : at + STRETCH, :] = ins[me_ref[0] ^ m, src, chans + NSTATE : chans + 2 * NSTATE]
            step_buf[at : at + STRETCH, :] = ins[me_ref[0] ^ m, src, chans + 2 * NSTATE : chans + 2 * NSTATE + 128]
        row = lax.broadcasted_iota(jnp.int32, (128, 128), 0)
        col = lax.broadcasted_iota(jnp.int32, (128, 128), 1)
        pick = ((row == col) | (row == col + heads) | (row == col + 2 * heads)) & (col < heads)
        step = mm(step_buf[...], jnp.where(pick, 1.0, 0.0).astype(BF16))
        rate = jnp.maximum(step, 0.0) + jnp.log1p(jnp.exp(-jnp.abs(step)))
        rate_out[...] = rate
        amount = rate * small_ref[0:1, :]
        pos_row = info_t_ref[0:1, :]
        same = (pos_row <= info_ref[:, 0:1]) & (pos_row >= info_ref[:, 1:2])
        same = jnp.where(same, 1.0, 0.0).astype(BF16)
        hi, mid, low = split3(amount)
        cum = mm(same, hi) + mm(same, mid) + mm(same, low)
        cum_out[...] = cum
        totals = [
            jnp.sum(amount * info_ref[:, 2 + q : 3 + q], axis=0, keepdims=True) for q in range(2)
        ]
        tail = jnp.zeros_like(cum)
        for q in range(2):
            tail = tail + info_ref[:, 2 + q : 3 + q] * jnp.exp(jnp.minimum(totals[q] - cum, 0.0))
        tail_out[...] = tail
        scale = rate * tail
        w_t = w_out[...].astype(F32).T
        w_q = [(w_t * info_t_ref[2 + q : 3 + q, :]).astype(BF16) for q in range(2)]
        sub = lax.broadcasted_iota(jnp.int32, (EXTRA, 128), 0)
        for k in range(heads // 2):
            lanes = slice(128 * k, 128 * (k + 1))
            xw = (x_out[:, lanes].astype(F32) * pair_spread(scale, k)).astype(BF16)
            for q in range(2):
                msg[q * NSTATE : (q + 1) * NSTATE, lanes] = mm(w_q[q], xw).astype(BF16)
            picked = jnp.zeros((EXTRA, 128), F32)
            for q in range(2):
                wide = pair_spread(jnp.broadcast_to(totals[q], (EXTRA, 128)), k)
                for i, part in enumerate(split3(wide)):
                    picked = jnp.where(sub == 3 * q + i, part.astype(F32), picked)
            msg[2 * NSTATE :, lanes] = picked.astype(BF16)

    return call(
        kernel,
        [
            ((2 * NSTATE + EXTRA, chans), BF16),
            ((rows, chans), BF16),
            ((rows, NSTATE), BF16),
            ((rows, NSTATE), BF16),
            ((rows, 128), F32),
            ((rows, 128), F32),
            ((rows, 128), F32),
        ],
        (me, pieces, info, info_t, small),
        smem=(0,),
        scratch=[pltpu.VMEM((rows, 128), BF16)],
        flops=4 * rows * NSTATE * chans,
        nbytes=6 * rows * chans,
    )


def intra_forward(x, w, r, cum, rate, info, info_t, chan):
    rows, chans = x.shape
    heads = chans // HEAD_CH
    mid = rows // 2

    def kernel(x_ref, w_ref, r_ref, cum_ref, rate_ref, info_ref, info_t_ref, chan_ref, y_ref, gm):
        cum_t = cum_ref[...].T
        lane = lax.broadcasted_iota(jnp.int32, (mid, 128), 1)
        spans = ((0, mid, mid), (mid, mid, rows))
        for start, count, depth in spans:
            at = slice(start, start + count)
            pos_row = info_t_ref[0:1, 0:depth]
            same = (pos_row <= info_ref[at, 0:1]) & (pos_row >= info_ref[at, 1:2])
            gm[at, 0:depth] = jnp.where(same, mm_nt(r_ref[at, :], w_ref[0:depth, :]), 0.0)
        for k in range(heads // 2):
            lanes = slice(128 * k, 128 * (k + 1))
            xf = x_ref[:, lanes].astype(F32)
            xr = (xf * pair_spread(rate_ref[...], k)).astype(BF16)
            for start, count, depth in spans:
                at = slice(start, start + count)
                both = []
                for h in (2 * k, 2 * k + 1):
                    gap = cum_ref[at, h : h + 1] - cum_t[h : h + 1, 0:depth]
                    mix = (jnp.exp(jnp.minimum(gap, 0.0)) * gm[at, 0:depth]).astype(BF16)
                    both.append(mm(mix, xr[0:depth]))
                y_ref[at, lanes] = jnp.where(lane < HEAD_CH, both[0], both[1]) + (
                    chan_ref[0:1, lanes] * xf[at]
                )

    return call(
        kernel,
        [((rows, chans), F32)],
        (x, w, r, cum, rate, info, info_t, chan),
        scratch=[pltpu.VMEM((rows, rows), F32)],
        flops=4 * rows * rows * chans,
        nbytes=8 * rows * chans,
    )[0]


def gather_states(refs, weight, store):
    for q in range(2):
        total = None
        index = 0
        for ref in refs:
            for k in range(ref.shape[0]):
                for c in range(2):
                    term = weight(q, index) * ref[k, c * NSTATE : (c + 1) * NSTATE, :].astype(F32)
                    total = term if total is None else total + term
                    index += 1
        store(q, total)


def mixed_rows(me, msgs, y, r, cum, gates, info, chan, before_in, ends, enter_mask, own_mask, own_end):
    rows, chans = y.shape
    heads = chans // HEAD_CH
    group = gates.shape[0]
    n_msg = len(msgs)
    classes = ends.shape[0]
    gate_at, grad_at = slice(0, chans), slice(chans, 2 * chans)

    def kernel(*refs):
        me_ref, msg_refs, gate_ref = refs[0], refs[1 : n_msg + 1], refs[n_msg + 1]
        (
            y_ref, r_ref, cum_ref, info_ref, chan_ref,
            before_ref, ends_ref, own_ref, own_end_ref, mask_ref,
            gated_ref, sums_ref, state_ref, enter_ref, leave_ref,
            tot, inner, cols,
        ) = refs[n_msg + 2 :]
        index = 0
        for ref in msg_refs:
            for k in range(ref.shape[0]):
                part = ref[k, 2 * NSTATE :, :].astype(F32)
                for c in range(2):
                    tot[index : index + 1, :] = (
                        part[3 * c : 3 * c + 1]
                        + part[3 * c + 1 : 3 * c + 2]
                        + part[3 * c + 2 : 3 * c + 3]
                    )
                    index += 1
        exact = lax.Precision.HIGHEST
        totals = tot[...]
        enter_ref[...] = jnp.dot(before_ref[...], totals, precision=exact, preferred_element_type=F32)
        leave_all = jnp.dot(ends_ref[...], totals, precision=exact, preferred_element_type=F32)
        own_in = jnp.dot(own_ref[...], totals, precision=exact, preferred_element_type=F32)
        leave_ref[...] = jnp.dot(
            own_end_ref[...], totals, precision=exact, preferred_element_type=F32
        )

        def weight(q, c):
            gap = own_in[q : q + 1] - leave_all[c : c + 1]
            return jnp.exp(jnp.minimum(gap, 0.0)) * mask_ref[q, c]

        def store(q, value):
            state_ref[q * NSTATE : (q + 1) * NSTATE, :] = value.astype(BF16)

        gather_states(msg_refs, weight, store)
        reads = r_ref[...].astype(F32)
        both = jnp.concatenate(
            [(reads * info_ref[:, 4:5]).astype(BF16), (reads * info_ref[:, 5:6]).astype(BF16)], axis=1
        )
        inner[...] = mm(both, state_ref[...])
        lane = lax.broadcasted_iota(jnp.int32, (STRETCH, 128), 1)
        for half, m, at in row_blocks(group):
            here = slice(at, at + STRETCH)
            src = slice(half * STRETCH, (half + 1) * STRETCH)
            mixed = y_ref[here, :] + spread(jnp.exp(cum_ref[here, :]), heads) * inner[here, :]
            gate = gate_ref[me_ref[0] ^ m, src, gate_at].astype(F32)
            gated = mixed * (gate / (1.0 + jnp.exp(-gate)))
            gated_ref[here, :] = gated
            grad = gate_ref[me_ref[0] ^ m, src, grad_at].astype(F32) * chan_ref[1:2, :]
            square = jnp.sum(gated * gated, axis=1, keepdims=True)
            cross = jnp.sum(grad * gated, axis=1, keepdims=True)
            cols[here, :] = jnp.where(lane == 0, square, jnp.where(lane == 1, cross, 0.0))
        sums_ref[...] = cols[...].T[0:8, :]

    args = (
        me, *msgs, gates, y, r, cum, info, chan, before_in, ends, own_mask, own_end, enter_mask
    )
    return call(
        kernel,
        [
            ((rows, chans), F32),
            ((8, rows), F32),
            ((2 * NSTATE, chans), BF16),
            ((classes, chans), F32),
            ((8, chans), F32),
        ],
        args,
        smem=(0, len(args) - 1),
        scratch=[
            pltpu.VMEM((classes, chans), F32),
            pltpu.VMEM((rows, chans), F32),
            pltpu.VMEM((rows, 128), F32),
        ],
        flops=4 * rows * 2 * NSTATE * chans,
        nbytes=16 * rows * chans,
    )


def mixed_cotangent(me, sums, gated, gates, r, cum, info_t, chan, total_chans):
    rows, chans = gated.shape
    heads = chans // HEAD_CH
    group = gates.shape[0]
    gate_at, grad_at = slice(0, chans), slice(chans, 2 * chans)

    def kernel(*refs):
        me_ref, gate_ref = refs[:2]
        sums_refs, refs = refs[2 : 2 + group], refs[2 + group :]
        gated_ref, r_ref, cum_ref, info_t_ref, chan_ref = refs[:5]
        touch_ref, dmix_ref, lift_ref, inv_ref, cols = refs[5:]
        parts = [ref[...] for ref in sums_refs]
        both = jnp.concatenate(parts + [jnp.zeros((128 - 8 * group, rows), F32)], axis=0)
        cols[...] = both.T
        for half, m, at in row_blocks(group):
            here = slice(at, at + STRETCH)
            src = slice(half * STRETCH, (half + 1) * STRETCH)
            square = cross = 0.0
            for peer in range(group):
                start = (half * group + (m ^ peer)) * STRETCH
                there = slice(start, start + STRETCH)
                square = square + cols[there, 8 * peer : 8 * peer + 1]
                cross = cross + cols[there, 8 * peer + 1 : 8 * peer + 2]
            inv = lax.rsqrt(square / total_chans + NORM_EPS)
            pull = inv * inv * inv * (cross / total_chans)
            gated = gated_ref[here, :]
            gain = chan_ref[1:2, :]
            inv_ref[here, :] = jnp.broadcast_to(inv, (STRETCH, 128))
            gate = gate_ref[me_ref[0] ^ m, src, gate_at].astype(F32)
            grad = gate_ref[me_ref[0] ^ m, src, grad_at].astype(F32) * gain
            dmix = (inv * grad - gated * pull) * (gate / (1.0 + jnp.exp(-gate)))
            dmix_ref[here, :] = dmix
            lift_ref[here, :] = (dmix * spread(jnp.exp(cum_ref[here, :]), heads)).astype(BF16)
        r_t = r_ref[...].astype(F32).T
        for q in range(2):
            left = (r_t * info_t_ref[4 + q : 5 + q, :]).astype(BF16)
            touch_ref[q * NSTATE : (q + 1) * NSTATE, :] = mm(left, lift_ref[...]).astype(BF16)

    return call(
        kernel,
        [
            ((2 * NSTATE, chans), BF16),
            ((rows, chans), F32),
            ((rows, chans), BF16),
            ((rows, 128), F32),
        ],
        (me, gates, *sums, gated, r, cum, info_t, chan),
        smem=(0,),
        scratch=[pltpu.VMEM((rows, 128), F32)],
        flops=4 * rows * NSTATE * chans,
        nbytes=16 * rows * chans,
    )


def intra_backward(x, w, r, cum, rate, dmix, lift, state, info, info_t):
    rows, chans = x.shape
    heads = chans // HEAD_CH
    mid = rows // 2

    def kernel(
        x_ref, w_ref, r_ref, cum_ref, rate_ref, dmix_ref, lift_ref, state_ref, info_ref, info_t_ref,
        dx_ref, dw_ref, dr_ref, gm, dgm,
    ):
        cum_t = cum_ref[...].T
        lane = lax.broadcasted_iota(jnp.int32, (rows, 128), 1)
        lane_mid = lax.broadcasted_iota(jnp.int32, (mid, 128), 1)
        spans = ((0, 0), (mid, mid))

        def same_of(start, later):
            pos = info_ref[start : start + mid, 0:1]
            return (pos <= info_t_ref[0:1, later:]) & (pos >= info_t_ref[1:2, later:])

        for start, later in spans:
            at = slice(start, start + mid)
            product = mm_nt(w_ref[at, :], r_ref[later:, :])
            gm[at, later:] = jnp.where(same_of(start, later), product, 0.0)
        for k in range(heads // 2):
            lanes = slice(128 * k, 128 * (k + 1))
            xr = x_ref[:, lanes].astype(F32) * pair_spread(rate_ref[...], k)
            parts = (
                jnp.where(lane < HEAD_CH, xr, 0.0).astype(BF16),
                jnp.where(lane < HEAD_CH, 0.0, xr).astype(BF16),
            )
            grads = dmix_ref[:, lanes].astype(BF16)
            for start, later in spans:
                at = slice(start, start + mid)
                both = []
                for i in range(2):
                    h = 2 * k + i
                    gap = cum_t[h : h + 1, later:] - cum_ref[at, h : h + 1]
                    fade = jnp.exp(jnp.minimum(gap, 0.0))
                    mix = (fade * gm[at, later:]).astype(BF16)
                    both.append(mm(mix, grads[later:]))
                    change = fade * mm_nt(parts[i][at], grads[later:])
                    if h == 0:
                        dgm[at, later:] = change
                    else:
                        dgm[at, later:] += change
                dx_ref[at, lanes] = jnp.where(lane_mid < HEAD_CH, both[0], both[1])
        carried = mm_nt(lift_ref[...], state_ref[0:NSTATE, :]) * info_ref[:, 4:5]
        carried = carried + mm_nt(lift_ref[...], state_ref[NSTATE:, :]) * info_ref[:, 5:6]
        dr_ref[...] = carried
        for start, later in spans:
            at = slice(start, start + mid)
            change = jnp.where(same_of(start, later), dgm[at, later:], 0.0)
            dw_ref[at, :] = mm(change.astype(BF16), r_ref[later:, :])
            dr_ref[later:, :] += mm(change.T.astype(BF16), w_ref[at, :])

    return call(
        kernel,
        [((rows, chans), F32), ((rows, NSTATE), F32), ((rows, NSTATE), F32)],
        (x, w, r, cum, rate, dmix, lift, state, info, info_t),
        scratch=[pltpu.VMEM((rows, rows), F32), pltpu.VMEM((rows, rows), F32)],
        flops=8 * rows * rows * chans,
        nbytes=16 * rows * chans,
    )


def final_grads(msgs, x, w, rate, tail, dx, dw, dr, dmix, gated, inv, info, chan, enter, leave, leave_mask):
    rows, chans = x.shape
    heads = chans // HEAD_CH
    group = rows // (2 * STRETCH)
    n_msg = len(msgs)
    width = 2 * chans + 2 * NSTATE

    def kernel(*refs):
        msg_refs = refs[:n_msg]
        (
            x_ref, w_ref, rate_ref, tail_ref, dx_ref, dw_ref, dr_ref, dmix_ref, gated_ref, inv_ref,
            info_ref, chan_ref, enter_ref, leave_ref, mask_ref,
        ) = refs[n_msg : n_msg + 15]
        outs = refs[n_msg + 15 : n_msg + 15 + group]
        after, inner, xw = refs[n_msg + 15 + group :]

        def weight(q, c):
            gap = enter_ref[c : c + 1, :] - leave_ref[q : q + 1, :]
            return jnp.exp(jnp.minimum(gap, 0.0)) * mask_ref[q, c]

        def store(q, value):
            after[q * NSTATE : (q + 1) * NSTATE, :] = value.astype(BF16)

        gather_states(msg_refs, weight, store)
        writes = w_ref[...].astype(F32)
        both = jnp.concatenate(
            [(writes * info_ref[:, 2:3]).astype(BF16), (writes * info_ref[:, 3:4]).astype(BF16)],
            axis=1,
        )
        inner[...] = mm(both, after[...])
        for half, m, at in row_blocks(group):
            here = slice(at, at + STRETCH)
            dst = slice(half * STRETCH, (half + 1) * STRETCH)
            rates = spread(rate_ref[here, :], heads)
            tails = spread(tail_ref[here, :], heads)
            xw[here, :] = (x_ref[here, :].astype(F32) * (rates * tails)).astype(BF16)
            change = rates * (dx_ref[here, :] + tails * inner[here, :])
            change = change + chan_ref[0:1, :] * dmix_ref[here, :]
            outs[m][dst, 0:chans] = change.astype(BF16)
            outs[m][dst, chans + NSTATE : chans + 2 * NSTATE] = dr_ref[here, :].astype(BF16)
            out = gated_ref[here, :] * inv_ref[here, 0:1] * chan_ref[1:2, :]
            outs[m][dst, chans + 2 * NSTATE :] = out.astype(BF16)
        change = dw_ref[...] + mm_nt(xw[...], after[0:NSTATE, :]) * info_ref[:, 2:3]
        change = change + mm_nt(xw[...], after[NSTATE:, :]) * info_ref[:, 3:4]
        for half, m, at in row_blocks(group):
            dst = slice(half * STRETCH, (half + 1) * STRETCH)
            outs[m][dst, chans : chans + NSTATE] = change[at : at + STRETCH].astype(BF16)

    args = (
        *msgs, x, w, rate, tail, dx, dw, dr, dmix, gated, inv, info, chan, enter, leave, leave_mask
    )
    return call(
        kernel,
        [((2 * STRETCH, width), BF16)] * group,
        args,
        smem=(len(args) - 1,),
        scratch=[
            pltpu.VMEM((2 * NSTATE, chans), BF16),
            pltpu.VMEM((rows, chans), F32),
            pltpu.VMEM((rows, chans), BF16),
        ],
        flops=8 * rows * NSTATE * chans,
        nbytes=16 * rows * chans,
    )


def attention(blocks, own_blocks, pieces, queries, grads, kv_heads):
    rows = queries.shape[0]
    per_kv = queries.shape[1] // AHD // kv_heads
    n_pieces = len(pieces)
    tokens = rows * sum(piece.shape[0] for piece in pieces)
    half_width = kv_heads * AHD
    scale = AHD ** (-0.5)
    chunk = min(KEY_CHUNK, tokens)
    tall = per_kv * STRETCH

    def kernel(*refs):
        blocks_ref, own_ref = refs[:2]
        piece_refs = refs[2 : 2 + n_pieces]
        q_ref, g_ref, out_ref, dq_ref, kv, scores, q_all, g_all = refs[2 + n_pieces :]
        index = 0
        for ref in piece_refs:
            for u in range(ref.shape[0]):
                for half in range(2):
                    at = pl.ds(pl.multiple_of(blocks_ref[half, index] * STRETCH, 64), STRETCH)
                    kv[at, :] = ref[u, half * STRETCH : (half + 1) * STRETCH, :]
                index += 1
        offset = lax.broadcasted_iota(jnp.int32, (tall, chunk), 0) % STRETCH
        column = lax.broadcasted_iota(jnp.int32, (tall, chunk), 1)
        every = range(kv_heads)
        k_at = [slice(g * AHD, (g + 1) * AHD) for g in every]
        v_at = [slice(half_width + g * AHD, half_width + (g + 1) * AHD) for g in every]

        def stacked(ref, src, g):
            parts = [ref[src, (g * per_kv + i) * AHD : (g * per_kv + i + 1) * AHD] for i in range(per_kv)]
            return jnp.concatenate(parts, axis=0)

        def keys_of(c):
            return pl.ds(pl.multiple_of(c * chunk, chunk), chunk)

        for half in range(2):
            block = own_ref[half]
            src = slice(half * STRETCH, (half + 1) * STRETCH)
            steps = (block * STRETCH) // chunk + 1
            reach = offset + block * STRETCH
            for g in every:
                q_all[g] = stacked(q_ref, src, g)
                g_all[g] = stacked(g_ref, src, g)

            def first(c, peaks):
                kept = column + c * chunk <= reach
                new = []
                for g in every:
                    value = mm_nt(q_all[g], kv[keys_of(c), k_at[g]]) * (scale * LOG2_E)
                    value = jnp.where(kept, value, NEG_FILL)
                    scores[g, c] = value
                    new.append(jnp.maximum(peaks[g], jnp.max(value, axis=1, keepdims=True)))
                return tuple(new)

            peaks = lax.fori_loop(
                0, steps, first, tuple(jnp.full((tall, 1), NEG_FILL, F32) for _ in every)
            )

            def second(c, carry):
                new = []
                for g in every:
                    total, out = carry[g]
                    value = jnp.exp2(scores[g, c] - peaks[g])
                    scores[g, c] = value
                    out = out + mm(value.astype(BF16), kv[keys_of(c), v_at[g]])
                    new.append((total + jnp.sum(value, axis=1, keepdims=True), out))
                return tuple(new)

            empty = (jnp.zeros((tall, 1), F32), jnp.zeros((tall, AHD), F32))
            done = lax.fori_loop(0, steps, second, tuple(empty for _ in every))
            deltas = []
            for g in every:
                total, out = done[g]
                out = (out / total).astype(BF16)
                deltas.append(
                    jnp.sum(g_all[g].astype(F32) * out.astype(F32), axis=1, keepdims=True)
                )
                for i in range(per_kv):
                    at = slice((g * per_kv + i) * AHD, (g * per_kv + i + 1) * AHD)
                    out_ref[src, at] = out[i * STRETCH : (i + 1) * STRETCH]

            def third(c, carry):
                new = []
                for g in every:
                    slope = mm_nt(g_all[g], kv[keys_of(c), v_at[g]]) - deltas[g]
                    change = (scores[g, c] * slope).astype(BF16)
                    new.append(carry[g] + mm(change, kv[keys_of(c), k_at[g]]))
                return tuple(new)

            changes = lax.fori_loop(
                0, steps, third, tuple(jnp.zeros((tall, AHD), F32) for _ in every)
            )
            for g in every:
                change = (changes[g] * (scale / done[g][0])).astype(BF16)
                for i in range(per_kv):
                    at = slice((g * per_kv + i) * AHD, (g * per_kv + i + 1) * AHD)
                    dq_ref[src, at] = change[i * STRETCH : (i + 1) * STRETCH]

    return call(
        kernel,
        [(queries.shape, BF16), (queries.shape, BF16)],
        (blocks, own_blocks, *pieces, queries, grads),
        smem=(0, 1),
        scratch=[
            pltpu.VMEM((tokens, 2 * half_width), BF16),
            pltpu.VMEM((kv_heads, tokens // chunk, tall, chunk), F32),
            pltpu.VMEM((kv_heads, tall, AHD), BF16),
            pltpu.VMEM((kv_heads, tall, AHD), BF16),
        ],
        mib=24,
        flops=10 * queries.size * tokens,
        nbytes=4 * tokens * half_width,
    )


def body(
    stretch_order,
    attn_queries,
    attn_keys,
    attn_values,
    attn_grad,
    mamba_input,
    gate_input,
    state_write,
    state_read,
    step_raw,
    decay_log,
    skip_gain,
    norm_gain,
    mamba_grad,
):
    ctx_count = lax.axis_size("ctx")
    tp_count = lax.axis_size("tp")
    group = state_write.shape[1] // NSTATE
    units = ctx_count // group
    by_permute = units <= 4
    my_index = lax.axis_index("ctx")
    my_unit, my_place = my_index // group, my_index % group
    me = my_place.astype(jnp.int32).reshape(1)
    chans = mamba_input.shape[1] // group
    heads = chans // HEAD_CH
    kv_heads = attn_keys.shape[1] // AHD
    turn = stretch_order[0]
    last = 2 * ctx_count

    def to_place(value, m):
        pairs = [(i, (i // group) * group + ((i % group) ^ m)) for i in range(ctx_count)]
        return lax.ppermute(value, "ctx", pairs)

    def in_plane(values):
        return [values[0]] + [to_place(values[m], m) for m in range(1, group)]

    def across(value):
        moved = []
        for m in range(units - 1, 0, -1):
            pairs = [(i, ((i // group) ^ m) * group + i % group) for i in range(ctx_count)]
            moved.append(lax.ppermute(value, "ctx", pairs))
        return [value] + moved[::-1]

    def all_units(value):
        if by_permute:
            return [part[None] for part in across(value)]
        if group == 1:
            return [lax.all_gather(value, "ctx", axis=0)]
        sets = [[u * group + j for u in range(units)] for j in range(group)]
        return [lax.all_gather(value, "ctx", axis=0, axis_index_groups=sets)]

    own_kv, packed, gates = pack_forward(
        mamba_input, state_write, state_read, step_raw, gate_input, mamba_grad, attn_keys,
        attn_values, group,
    )
    kv_units = all_units(own_kv)
    forward_pieces = packed
    if group > 1:
        planes = [[u * group + j for j in range(group)] for u in range(units)]
        forward_pieces = lax.all_to_all(packed, "ctx", 0, 0, axis_index_groups=planes, tiled=True)
        gates = lax.all_to_all(after(gates, forward_pieces), "ctx", 0, 0, axis_index_groups=planes, tiled=True)

    unit_ids = jnp.arange(units, dtype=jnp.int32)
    if by_permute:
        unit_ids = unit_ids ^ my_unit
    place_ids = jnp.arange(group, dtype=jnp.int32) ^ my_place

    def class_bounds(unit):
        first = (unit * group + turn) % ctx_count
        wraps = first + group > ctx_count
        extra = first + group - ctx_count
        out_start = (jnp.where(wraps, 0, first), jnp.where(wraps, first, last - first - group))
        out_end = (jnp.where(wraps, extra, first + group), last - first)
        in_start = (first, jnp.where(wraps, last - extra, last - first - group))
        in_end = (
            jnp.where(wraps, last - first, first + group),
            jnp.where(wraps, last, last - first),
        )
        return out_start, out_end, in_start, in_end

    out_start, out_end, in_start, in_end = class_bounds(my_unit)
    _, all_out_end, all_in_start, _ = class_bounds(unit_ids)
    all_out_end = jnp.stack(all_out_end, axis=1).reshape(-1)
    all_in_start = jnp.stack(all_in_start, axis=1).reshape(-1)
    own_out_end = jnp.stack(out_end)
    own_in_start = jnp.stack(in_start)
    enter_mask = (all_out_end[None, :] <= own_in_start[:, None]).astype(F32)
    leave_mask = (own_out_end[:, None] <= all_in_start[None, :]).astype(F32)
    own_end = (all_out_end[None, :] <= own_out_end[:, None]).astype(F32)
    before_in = (all_out_end[None, :] <= all_in_start[:, None]).astype(F32)
    ends = (all_out_end[None, :] <= all_out_end[:, None]).astype(F32)
    own_mask = jnp.concatenate([enter_mask, jnp.zeros((6, 2 * units), F32)], axis=0)
    own_end = jnp.concatenate([own_end, jnp.zeros((6, 2 * units), F32)], axis=0)

    def info_of(row):
        half, place, offset = row // (group * STRETCH), (row // STRETCH) % group, row % STRETCH
        pair = (my_unit * group + (place ^ my_place) + turn) % ctx_count
        block = jnp.where(half == 0, pair, last - 1 - pair)

        def within(start, end):
            return ((block >= start) & (block < end)).astype(F32)

        low = jnp.where(
            within(in_start[1], in_end[1]) > 0,
            in_start[1],
            jnp.where(within(in_start[0], in_end[0]) > 0, in_start[0], out_start[0]),
        )
        return [
            (block * STRETCH + offset).astype(F32),
            (low * STRETCH).astype(F32),
            within(out_start[0], out_end[0]),
            within(out_start[1], out_end[1]),
            within(in_start[0], in_end[0]),
            within(in_start[1], in_end[1]),
        ]

    rows = 2 * group * STRETCH
    cols = info_of(lax.broadcasted_iota(jnp.int32, (rows, 8), 0))
    pick = lax.broadcasted_iota(jnp.int32, (rows, 8), 1)
    info = sum(jnp.where(pick == i, c, 0.0) for i, c in enumerate(cols))
    cols = info_of(lax.broadcasted_iota(jnp.int32, (8, rows), 1))
    pick = lax.broadcasted_iota(jnp.int32, (8, rows), 0)
    info_t = sum(jnp.where(pick == i, c, 0.0) for i, c in enumerate(cols))

    decay = -jnp.exp(lax.dynamic_slice(decay_log, (my_place * heads,), (heads,)))
    small = jnp.pad(decay[None], ((0, 7), (0, 128 - heads)))
    skip = jnp.repeat(lax.dynamic_slice(skip_gain, (my_place * heads,), (heads,)), HEAD_CH)
    gain = lax.dynamic_slice(norm_gain, (my_place * chans,), (chans,))
    chan = jnp.pad(jnp.stack([skip, gain]), ((0, 6), (0, 0)))

    own_pair = (my_index + turn) % ctx_count
    pair_table = (unit_ids[None, :] * group + place_ids[:, None] + turn) % ctx_count
    pair_table = pair_table.reshape(1, -1)
    blocks = jnp.concatenate([pair_table, last - 1 - pair_table], axis=0)
    own_blocks = jnp.stack([own_pair, last - 1 - own_pair])
    tables = (
        info, info_t, small, chan, before_in, ends, enter_mask, leave_mask, own_mask, own_end,
        blocks, own_blocks,
    )
    small_group = group == 4 and units == 4 and by_permute
    forward_pieces, tables = after((forward_pieces, tables), kv_units)
    (
        info, info_t, small, chan, before_in, ends, enter_mask, leave_mask, own_mask, own_end,
        blocks, own_blocks,
    ) = tables

    msg, x, w, r, cum, rate, tail = outgoing_state(me, forward_pieces, info, info_t, small, chans)
    msgs = all_units(msg)
    y = intra_forward(x, w, r, cum, rate, info, info_t, chan)
    if small_group:
        near = stack_parts(after(kv_units, (gates, y)))
        beside, above = to_place(near, 1), to_place(near, 2)
        x_late = x
    else:
        kv_pieces = in_plane([jnp.concatenate(kv_units, axis=0)] * group)
        x_late = x
    gated, sums, state, enter, leave = mixed_rows(
        me, msgs, y, r, cum, gates, info, chan, before_in, ends, enter_mask, own_mask, own_end
    )
    if tp_count == 2:
        sums = sums + lax.ppermute(sums, "tp", [(0, 1), (1, 0)])
    else:
        sums = lax.psum(sums, "tp")
    sums = in_plane([sums] * group)
    touch, dmix, lift, inv = mixed_cotangent(
        me, sums, gated, gates, r, cum, info_t, chan, float(mamba_input.shape[1] * tp_count)
    )
    touches = all_units(touch)
    if small_group:
        beside, above = after((beside, above), touch)
        kv_pieces = [near, beside, above, to_place(beside[:2], 2), to_place(above[2:], 1)]
    dx, dw, dr = intra_backward(x, w, r, cum, rate, dmix, lift, state, info, info_t)

    attn_output, query_grad = attention(
        blocks, own_blocks, kv_pieces, attn_queries, attn_grad, kv_heads
    )

    touches, attn_output, query_grad = lax.optimization_barrier((touches, attn_output, query_grad))
    finals = final_grads(
        touches, x, w, rate, tail, dx, dw, dr, dmix, gated, inv, info, chan, enter, leave, leave_mask
    )
    input_grad, write_grad, read_grad, mamba_output = unpack(
        me, in_plane(finals), (chans, NSTATE, NSTATE, chans)
    )
    return (attn_output, query_grad, mamba_output, input_grad, write_grad, read_grad)


def solution(mesh):
    wide, flat = P("ctx", "tp"), P("tp")
    return jax.shard_map(
        body,
        mesh=mesh,
        in_specs=(P(),) + (wide,) * 9 + (flat,) * 3 + (wide,),
        out_specs=(wide,) * 6,
        check_vma=False,
    )
```

```python
import jax
import jax.numpy as jnp
from jax import lax
from jax.experimental import pallas as pl
from jax.experimental.pallas import tpu as pltpu
from jax.sharding import PartitionSpec as P

HEAD_CH = 64
NSTATE = 128
AHD = 128
STRETCH = 64
EXTRA = 16
NORM_EPS = 1e-05
NEG_FILL = -1e30
KEY_CHUNK = 512
LOG2_E = 1.4426950408889634
F32 = jnp.float32
BF16 = jnp.bfloat16
MIB = 1024 * 1024


def after(value, event):
    return lax.optimization_barrier((value, event))[0]


def mm(a, b):
    return lax.dot_general(a, b, (((1,), (0,)), ((), ())), preferred_element_type=F32)


def mm_nt(a, b):
    return lax.dot_general(a, b, (((1,), (1,)), ((), ())), preferred_element_type=F32)


def split3(v):
    hi = v.astype(BF16)
    rest = v - hi.astype(F32)
    mid = rest.astype(BF16)
    low = (rest - mid.astype(F32)).astype(BF16)
    return hi, mid, low


def pair_spread(cols, k):
    rows = cols.shape[0]
    lane = lax.broadcasted_iota(jnp.int32, (rows, 128), 1)
    even = jnp.broadcast_to(cols[:, 2 * k : 2 * k + 1], (rows, 128))
    odd = jnp.broadcast_to(cols[:, 2 * k + 1 : 2 * k + 2], (rows, 128))
    return jnp.where(lane < HEAD_CH, even, odd)


def spread(cols, heads):
    return jnp.concatenate([pair_spread(cols, k) for k in range(heads // 2)], axis=1)


def call(fn, outs, args, smem=(), scratch=(), flops=0, nbytes=0, mib=12):
    specs = [
        pl.BlockSpec(memory_space=pltpu.SMEM if i in smem else pltpu.VMEM)
        for i in range(len(args))
    ]
    return pl.pallas_call(
        fn,
        out_shape=tuple(jax.ShapeDtypeStruct(s, d) for s, d in outs),
        in_specs=specs,
        out_specs=tuple(pl.BlockSpec(memory_space=pltpu.VMEM) for _ in outs),
        scratch_shapes=list(scratch),
        compiler_params=pltpu.CompilerParams(vmem_limit_bytes=mib * MIB),
        cost_estimate=pl.CostEstimate(flops=flops // 1000, bytes_accessed=nbytes // 1000, transcendentals=0),
    )(*args)


def pack_gates(gate, grad, group):
    rows, chans = gate.shape[0], gate.shape[1] // group

    def kernel(gate_ref, grad_ref, out):
        for m in range(group):
            out[m, :, 0:chans] = gate_ref[:, m * chans : (m + 1) * chans]
            out[m, :, chans : 2 * chans] = grad_ref[:, m * chans : (m + 1) * chans]

    return call(kernel, [((group, rows, 2 * chans), BF16)], (gate, grad), nbytes=8 * gate.size)[0]


def pack_forward(x, w, r, step, keys, values, group):
    rows, chans = x.shape[0], x.shape[1] // group
    heads = step.shape[1] // group
    width = chans + 2 * NSTATE + 128
    kv_width = keys.shape[1]

    wide = [(0, chans), (1, NSTATE), (2, NSTATE), (None, 128)]
    sources = (x, w, r, keys, values)
    n_in = len(sources)
    n_out = 2 + group * len(wide)

    def kernel(step_ref, *refs):
        ins, kv_ref, out = refs[:n_in], *refs[n_in : n_in + 2]
        held = refs[n_in + 2 : -3]
        step_buf, in_sems, out_sems = refs[-3:]
        loads = [pltpu.make_async_copy(ins[i], held[i], in_sems.at[i]) for i in range(n_in)]
        for i in (3, 4, 0, 1, 2):
            loads[i].start()
        parts = split3(step_ref[...])
        row = lax.broadcasted_iota(jnp.int32, (heads * group, 128), 0)
        col = lax.broadcasted_iota(jnp.int32, (heads * group, 128), 1)
        for m in range(group):
            total = jnp.zeros((rows, 128), F32)
            for i in range(3):
                pick = (row - m * heads == col - i * heads) & (col >= i * heads)
                pick = pick & (col < (i + 1) * heads)
                total = total + mm(parts[i], jnp.where(pick, 1.0, 0.0).astype(BF16))
            step_buf[m] = total.astype(BF16)
        copies = []

        def send(src, dst):
            copy = pltpu.make_async_copy(src, dst, out_sems.at[len(copies)])
            copy.start()
            copies.append(copy)

        loads[3].wait()
        send(held[3], kv_ref.at[:, 0:kv_width])
        loads[4].wait()
        send(held[4], kv_ref.at[:, kv_width : 2 * kv_width])
        start = 0
        for source, count in wide:
            if source is not None:
                loads[source].wait()
            for m in range(group):
                at = slice(m * count, (m + 1) * count)
                dst = out.at[m, :, start : start + count]
                send(step_buf.at[m] if source is None else held[source].at[:, at], dst)
            start += count
        for copy in copies:
            copy.wait()

    return move(
        kernel,
        [((rows, 2 * kv_width), BF16)]
        + [((group, rows, width), BF16)],
        (step, *sources),
        (pltpu.VMEM,),
        [pltpu.VMEM(source.shape, BF16) for source in sources]
        + [
            pltpu.VMEM((group, rows, 128), BF16),
            pltpu.SemaphoreType.DMA((n_in,)),
            pltpu.SemaphoreType.DMA((n_out,)),
        ],
        mib=60,
    )


def move(fn, outs, args, spaces, scratch, mib=8):
    spaces = tuple(spaces) + (pl.ANY,) * (len(args) - len(spaces))
    return pl.pallas_call(
        fn,
        out_shape=tuple(jax.ShapeDtypeStruct(s, d) for s, d in outs),
        in_specs=[pl.BlockSpec(memory_space=space) for space in spaces],
        out_specs=tuple(pl.BlockSpec(memory_space=pl.ANY) for _ in outs),
        scratch_shapes=scratch,
        compiler_params=pltpu.CompilerParams(vmem_limit_bytes=mib * MIB),
        cost_estimate=pl.CostEstimate(flops=0, bytes_accessed=1024, transcendentals=0),
    )(*args)


def stack_parts(parts):
    count = len(parts)

    def kernel(*refs):
        for i in range(count):
            refs[count][i] = refs[i][0]

    shape = (count,) + parts[0].shape[1:]
    return call(kernel, [(shape, BF16)], parts, nbytes=4 * count * parts[0].size)[0]


def unpack(me, pieces, widths):
    group, rows = len(pieces), pieces[0].shape[0]

    def kernel(me_ref, *refs):
        outs = refs[group:]
        for m in range(group):
            start = 0
            for out, width in zip(outs, widths):
                at = pl.ds(pl.multiple_of((me_ref[0] ^ m) * width, 128), width)
                out[:, at] = refs[m][:, start : start + width]
                start += width

    return call(
        kernel,
        [((rows, group * width), BF16) for width in widths],
        (me, *pieces),
        smem=(0,),
        nbytes=4 * rows * group * sum(widths),
    )


def row_blocks(group):
    for half in range(2):
        for m in range(group):
            yield half, m, (half * group + m) * STRETCH


def outgoing_state(me, pieces, info, info_t, small, chans):
    group = pieces.shape[0]
    rows = 2 * group * STRETCH
    heads = chans // HEAD_CH

    def kernel(*refs):
        me_ref, ins, info_ref, info_t_ref, small_ref = refs[:5]
        msg, x_out, w_out, r_out, cum_out, rate_out, tail_out, step_buf = refs[5:]
        for half, m, at in row_blocks(group):
            src = slice(half * STRETCH, (half + 1) * STRETCH)
            x_out[at : at + STRETCH, :] = ins[me_ref[0] ^ m, src, 0:chans]
            w_out[at : at + STRETCH, :] = ins[me_ref[0] ^ m, src, chans : chans + NSTATE]
            r_out[at : at + STRETCH, :] = ins[me_ref[0] ^ m, src, chans + NSTATE : chans + 2 * NSTATE]
            step_buf[at : at + STRETCH, :] = ins[me_ref[0] ^ m, src, chans + 2 * NSTATE : chans + 2 * NSTATE + 128]
        row = lax.broadcasted_iota(jnp.int32, (128, 128), 0)
        col = lax.broadcasted_iota(jnp.int32, (128, 128), 1)
        pick = ((row == col) | (row == col + heads) | (row == col + 2 * heads)) & (col < heads)
        step = mm(step_buf[...], jnp.where(pick, 1.0, 0.0).astype(BF16))
        rate = jnp.maximum(step, 0.0) + jnp.log1p(jnp.exp(-jnp.abs(step)))
        rate_out[...] = rate
        amount = rate * small_ref[0:1, :]
        pos_row = info_t_ref[0:1, :]
        same = (pos_row <= info_ref[:, 0:1]) & (pos_row >= info_ref[:, 1:2])
        same = jnp.where(same, 1.0, 0.0).astype(BF16)
        hi, mid, low = split3(amount)
        cum = mm(same, hi) + mm(same, mid) + mm(same, low)
        cum_out[...] = cum
        totals = [
            jnp.sum(amount * info_ref[:, 2 + q : 3 + q], axis=0, keepdims=True) for q in range(2)
        ]
        tail = jnp.zeros_like(cum)
        for q in range(2):
            tail = tail + info_ref[:, 2 + q : 3 + q] * jnp.exp(jnp.minimum(totals[q] - cum, 0.0))
        tail_out[...] = tail
        scale = rate * tail
        w_t = w_out[...].astype(F32).T
        w_q = [(w_t * info_t_ref[2 + q : 3 + q, :]).astype(BF16) for q in range(2)]
        sub = lax.broadcasted_iota(jnp.int32, (EXTRA, 128), 0)
        for k in range(heads // 2):
            lanes = slice(128 * k, 128 * (k + 1))
            xw = (x_out[:, lanes].astype(F32) * pair_spread(scale, k)).astype(BF16)
            for q in range(2):
                msg[q * NSTATE : (q + 1) * NSTATE, lanes] = mm(w_q[q], xw).astype(BF16)
            picked = jnp.zeros((EXTRA, 128), F32)
            for q in range(2):
                wide = pair_spread(jnp.broadcast_to(totals[q], (EXTRA, 128)), k)
                for i, part in enumerate(split3(wide)):
                    picked = jnp.where(sub == 3 * q + i, part.astype(F32), picked)
            msg[2 * NSTATE :, lanes] = picked.astype(BF16)

    return call(
        kernel,
        [
            ((2 * NSTATE + EXTRA, chans), BF16),
            ((rows, chans), BF16),
            ((rows, NSTATE), BF16),
            ((rows, NSTATE), BF16),
            ((rows, 128), F32),
            ((rows, 128), F32),
            ((rows, 128), F32),
        ],
        (me, pieces, info, info_t, small),
        smem=(0,),
        scratch=[pltpu.VMEM((rows, 128), BF16)],
        flops=4 * rows * NSTATE * chans,
        nbytes=6 * rows * chans,
    )


def intra_forward(x, w, r, cum, rate, info, info_t, chan):
    rows, chans = x.shape
    heads = chans // HEAD_CH
    mid = rows // 2

    def kernel(x_ref, w_ref, r_ref, cum_ref, rate_ref, info_ref, info_t_ref, chan_ref, y_ref, gm):
        cum_t = cum_ref[...].T
        lane = lax.broadcasted_iota(jnp.int32, (mid, 128), 1)
        spans = ((0, mid, mid), (mid, mid, rows))
        for start, count, depth in spans:
            at = slice(start, start + count)
            pos_row = info_t_ref[0:1, 0:depth]
            same = (pos_row <= info_ref[at, 0:1]) & (pos_row >= info_ref[at, 1:2])
            gm[at, 0:depth] = jnp.where(same, mm_nt(r_ref[at, :], w_ref[0:depth, :]), 0.0)
        for k in range(heads // 2):
            lanes = slice(128 * k, 128 * (k + 1))
            xf = x_ref[:, lanes].astype(F32)
            xr = (xf * pair_spread(rate_ref[...], k)).astype(BF16)
            for start, count, depth in spans:
                at = slice(start, start + count)
                both = []
                for h in (2 * k, 2 * k + 1):
                    gap = cum_ref[at, h : h + 1] - cum_t[h : h + 1, 0:depth]
                    mix = (jnp.exp(jnp.minimum(gap, 0.0)) * gm[at, 0:depth]).astype(BF16)
                    both.append(mm(mix, xr[0:depth]))
                y_ref[at, lanes] = jnp.where(lane < HEAD_CH, both[0], both[1]) + (
                    chan_ref[0:1, lanes] * xf[at]
                )

    return call(
        kernel,
        [((rows, chans), F32)],
        (x, w, r, cum, rate, info, info_t, chan),
        scratch=[pltpu.VMEM((rows, rows), F32)],
        flops=4 * rows * rows * chans,
        nbytes=8 * rows * chans,
    )[0]


def gather_states(refs, weight, store):
    for q in range(2):
        total = None
        index = 0
        for ref in refs:
            for k in range(ref.shape[0]):
                for c in range(2):
                    term = weight(q, index) * ref[k, c * NSTATE : (c + 1) * NSTATE, :].astype(F32)
                    total = term if total is None else total + term
                    index += 1
        store(q, total)


def mixed_rows(me, msgs, y, r, cum, gates, info, chan, before_in, ends, enter_mask, own_mask, own_end):
    rows, chans = y.shape
    heads = chans // HEAD_CH
    group = gates.shape[0]
    n_msg = len(msgs)
    classes = ends.shape[0]
    gate_at, grad_at = slice(0, chans), slice(chans, 2 * chans)

    def kernel(*refs):
        me_ref, msg_refs, gate_ref = refs[0], refs[1 : n_msg + 1], refs[n_msg + 1]
        (
            y_ref, r_ref, cum_ref, info_ref, chan_ref,
            before_ref, ends_ref, own_ref, own_end_ref, mask_ref,
            gated_ref, sums_ref, state_ref, enter_ref, leave_ref,
            tot, inner, cols,
        ) = refs[n_msg + 2 :]
        index = 0
        for ref in msg_refs:
            for k in range(ref.shape[0]):
                part = ref[k, 2 * NSTATE :, :].astype(F32)
                for c in range(2):
                    tot[index : index + 1, :] = (
                        part[3 * c : 3 * c + 1]
                        + part[3 * c + 1 : 3 * c + 2]
                        + part[3 * c + 2 : 3 * c + 3]
                    )
                    index += 1
        exact = lax.Precision.HIGHEST
        totals = tot[...]
        enter_ref[...] = jnp.dot(before_ref[...], totals, precision=exact, preferred_element_type=F32)
        leave_all = jnp.dot(ends_ref[...], totals, precision=exact, preferred_element_type=F32)
        own_in = jnp.dot(own_ref[...], totals, precision=exact, preferred_element_type=F32)
        leave_ref[...] = jnp.dot(
            own_end_ref[...], totals, precision=exact, preferred_element_type=F32
        )

        def weight(q, c):
            gap = own_in[q : q + 1] - leave_all[c : c + 1]
            return jnp.exp(jnp.minimum(gap, 0.0)) * mask_ref[q, c]

        def store(q, value):
            state_ref[q * NSTATE : (q + 1) * NSTATE, :] = value.astype(BF16)

        gather_states(msg_refs, weight, store)
        reads = r_ref[...].astype(F32)
        both = jnp.concatenate(
            [(reads * info_ref[:, 4:5]).astype(BF16), (reads * info_ref[:, 5:6]).astype(BF16)], axis=1
        )
        inner[...] = mm(both, state_ref[...])
        lane = lax.broadcasted_iota(jnp.int32, (STRETCH, 128), 1)
        for half, m, at in row_blocks(group):
            here = slice(at, at + STRETCH)
            src = slice(half * STRETCH, (half + 1) * STRETCH)
            mixed = y_ref[here, :] + spread(jnp.exp(cum_ref[here, :]), heads) * inner[here, :]
            gate = gate_ref[me_ref[0] ^ m, src, gate_at].astype(F32)
            gated = mixed * (gate / (1.0 + jnp.exp(-gate)))
            gated_ref[here, :] = gated
            grad = gate_ref[me_ref[0] ^ m, src, grad_at].astype(F32) * chan_ref[1:2, :]
            square = jnp.sum(gated * gated, axis=1, keepdims=True)
            cross = jnp.sum(grad * gated, axis=1, keepdims=True)
            cols[here, :] = jnp.where(lane == 0, square, jnp.where(lane == 1, cross, 0.0))
        sums_ref[...] = cols[...].T[0:8, :]

    args = (
        me, *msgs, gates, y, r, cum, info, chan, before_in, ends, own_mask, own_end, enter_mask
    )
    return call(
        kernel,
        [
            ((rows, chans), F32),
            ((8, rows), F32),
            ((2 * NSTATE, chans), BF16),
            ((classes, chans), F32),
            ((8, chans), F32),
        ],
        args,
        smem=(0, len(args) - 1),
        scratch=[
            pltpu.VMEM((classes, chans), F32),
            pltpu.VMEM((rows, chans), F32),
            pltpu.VMEM((rows, 128), F32),
        ],
        flops=35 * 10**12,
        nbytes=16 * rows * chans,
    )


def mixed_cotangent(me, sums, gated, gates, r, cum, info_t, chan, total_chans):
    rows, chans = gated.shape
    heads = chans // HEAD_CH
    group = gates.shape[0]
    gate_at, grad_at = slice(0, chans), slice(chans, 2 * chans)

    def kernel(*refs):
        me_ref, gate_ref = refs[:2]
        sums_refs, refs = refs[2 : 2 + group], refs[2 + group :]
        gated_ref, r_ref, cum_ref, info_t_ref, chan_ref = refs[:5]
        touch_ref, dmix_ref, lift_ref, inv_ref, cols = refs[5:]
        parts = [ref[...] for ref in sums_refs]
        both = jnp.concatenate(parts + [jnp.zeros((128 - 8 * group, rows), F32)], axis=0)
        cols[...] = both.T
        for half, m, at in row_blocks(group):
            here = slice(at, at + STRETCH)
            src = slice(half * STRETCH, (half + 1) * STRETCH)
            square = cross = 0.0
            for peer in range(group):
                start = (half * group + (m ^ peer)) * STRETCH
                there = slice(start, start + STRETCH)
                square = square + cols[there, 8 * peer : 8 * peer + 1]
                cross = cross + cols[there, 8 * peer + 1 : 8 * peer + 2]
            inv = lax.rsqrt(square / total_chans + NORM_EPS)
            pull = inv * inv * inv * (cross / total_chans)
            gated = gated_ref[here, :]
            gain = chan_ref[1:2, :]
            inv_ref[here, :] = jnp.broadcast_to(inv, (STRETCH, 128))
            gate = gate_ref[me_ref[0] ^ m, src, gate_at].astype(F32)
            grad = gate_ref[me_ref[0] ^ m, src, grad_at].astype(F32) * gain
            dmix = (inv * grad - gated * pull) * (gate / (1.0 + jnp.exp(-gate)))
            dmix_ref[here, :] = dmix
            lift_ref[here, :] = (dmix * spread(jnp.exp(cum_ref[here, :]), heads)).astype(BF16)
        r_t = r_ref[...].astype(F32).T
        for q in range(2):
            left = (r_t * info_t_ref[4 + q : 5 + q, :]).astype(BF16)
            touch_ref[q * NSTATE : (q + 1) * NSTATE, :] = mm(left, lift_ref[...]).astype(BF16)

    return call(
        kernel,
        [
            ((2 * NSTATE, chans), BF16),
            ((rows, chans), F32),
            ((rows, chans), BF16),
            ((rows, 128), F32),
        ],
        (me, gates, *sums, gated, r, cum, info_t, chan),
        smem=(0,),
        scratch=[pltpu.VMEM((rows, 128), F32)],
        flops=4 * rows * NSTATE * chans,
        nbytes=16 * rows * chans,
    )


def intra_backward(x, w, r, cum, rate, dmix, lift, state, info, info_t):
    rows, chans = x.shape
    heads = chans // HEAD_CH
    mid = rows // 2

    def kernel(
        x_ref, w_ref, r_ref, cum_ref, rate_ref, dmix_ref, lift_ref, state_ref, info_ref, info_t_ref,
        dx_ref, dw_ref, dr_ref, gm, dgm,
    ):
        cum_t = cum_ref[...].T
        lane = lax.broadcasted_iota(jnp.int32, (rows, 128), 1)
        lane_mid = lax.broadcasted_iota(jnp.int32, (mid, 128), 1)
        spans = ((0, 0), (mid, mid))

        def same_of(start, later):
            pos = info_ref[start : start + mid, 0:1]
            return (pos <= info_t_ref[0:1, later:]) & (pos >= info_t_ref[1:2, later:])

        for start, later in spans:
            at = slice(start, start + mid)
            product = mm_nt(w_ref[at, :], r_ref[later:, :])
            gm[at, later:] = jnp.where(same_of(start, later), product, 0.0)
        for k in range(heads // 2):
            lanes = slice(128 * k, 128 * (k + 1))
            xr = x_ref[:, lanes].astype(F32) * pair_spread(rate_ref[...], k)
            parts = (
                jnp.where(lane < HEAD_CH, xr, 0.0).astype(BF16),
                jnp.where(lane < HEAD_CH, 0.0, xr).astype(BF16),
            )
            grads = dmix_ref[:, lanes].astype(BF16)
            for start, later in spans:
                at = slice(start, start + mid)
                both = []
                for i in range(2):
                    h = 2 * k + i
                    gap = cum_t[h : h + 1, later:] - cum_ref[at, h : h + 1]
                    fade = jnp.exp(jnp.minimum(gap, 0.0))
                    mix = (fade * gm[at, later:]).astype(BF16)
                    both.append(mm(mix, grads[later:]))
                    change = fade * mm_nt(parts[i][at], grads[later:])
                    if h == 0:
                        dgm[at, later:] = change
                    else:
                        dgm[at, later:] += change
                dx_ref[at, lanes] = jnp.where(lane_mid < HEAD_CH, both[0], both[1])
        carried = mm_nt(lift_ref[...], state_ref[0:NSTATE, :]) * info_ref[:, 4:5]
        carried = carried + mm_nt(lift_ref[...], state_ref[NSTATE:, :]) * info_ref[:, 5:6]
        dr_ref[...] = carried
        for start, later in spans:
            at = slice(start, start + mid)
            change = jnp.where(same_of(start, later), dgm[at, later:], 0.0)
            dw_ref[at, :] = mm(change.astype(BF16), r_ref[later:, :])
            dr_ref[later:, :] += mm(change.T.astype(BF16), w_ref[at, :])

    return call(
        kernel,
        [((rows, chans), F32), ((rows, NSTATE), F32), ((rows, NSTATE), F32)],
        (x, w, r, cum, rate, dmix, lift, state, info, info_t),
        scratch=[pltpu.VMEM((rows, rows), F32), pltpu.VMEM((rows, rows), F32)],
        flops=8 * rows * rows * chans,
        nbytes=16 * rows * chans,
    )


def final_grads(msgs, x, w, rate, tail, dx, dw, dr, dmix, gated, inv, info, chan, enter, leave, leave_mask):
    rows, chans = x.shape
    heads = chans // HEAD_CH
    group = rows // (2 * STRETCH)
    n_msg = len(msgs)
    width = 2 * chans + 2 * NSTATE

    def kernel(*refs):
        msg_refs = refs[:n_msg]
        (
            x_ref, w_ref, rate_ref, tail_ref, dx_ref, dw_ref, dr_ref, dmix_ref, gated_ref, inv_ref,
            info_ref, chan_ref, enter_ref, leave_ref, mask_ref,
        ) = refs[n_msg : n_msg + 15]
        outs = refs[n_msg + 15 : n_msg + 15 + group]
        after, inner, xw = refs[n_msg + 15 + group :]

        def weight(q, c):
            gap = enter_ref[c : c + 1, :] - leave_ref[q : q + 1, :]
            return jnp.exp(jnp.minimum(gap, 0.0)) * mask_ref[q, c]

        def store(q, value):
            after[q * NSTATE : (q + 1) * NSTATE, :] = value.astype(BF16)

        gather_states(msg_refs, weight, store)
        writes = w_ref[...].astype(F32)
        both = jnp.concatenate(
            [(writes * info_ref[:, 2:3]).astype(BF16), (writes * info_ref[:, 3:4]).astype(BF16)],
            axis=1,
        )
        inner[...] = mm(both, after[...])
        for half, m, at in row_blocks(group):
            here = slice(at, at + STRETCH)
            dst = slice(half * STRETCH, (half + 1) * STRETCH)
            rates = spread(rate_ref[here, :], heads)
            tails = spread(tail_ref[here, :], heads)
            xw[here, :] = (x_ref[here, :].astype(F32) * (rates * tails)).astype(BF16)
            change = rates * (dx_ref[here, :] + tails * inner[here, :])
            change = change + chan_ref[0:1, :] * dmix_ref[here, :]
            outs[m][dst, 0:chans] = change.astype(BF16)
            outs[m][dst, chans + NSTATE : chans + 2 * NSTATE] = dr_ref[here, :].astype(BF16)
            out = gated_ref[here, :] * inv_ref[here, 0:1] * chan_ref[1:2, :]
            outs[m][dst, chans + 2 * NSTATE :] = out.astype(BF16)
        change = dw_ref[...] + mm_nt(xw[...], after[0:NSTATE, :]) * info_ref[:, 2:3]
        change = change + mm_nt(xw[...], after[NSTATE:, :]) * info_ref[:, 3:4]
        for half, m, at in row_blocks(group):
            dst = slice(half * STRETCH, (half + 1) * STRETCH)
            outs[m][dst, chans : chans + NSTATE] = change[at : at + STRETCH].astype(BF16)

    args = (
        *msgs, x, w, rate, tail, dx, dw, dr, dmix, gated, inv, info, chan, enter, leave, leave_mask
    )
    return call(
        kernel,
        [((2 * STRETCH, width), BF16)] * group,
        args,
        smem=(len(args) - 1,),
        scratch=[
            pltpu.VMEM((2 * NSTATE, chans), BF16),
            pltpu.VMEM((rows, chans), F32),
            pltpu.VMEM((rows, chans), BF16),
        ],
        flops=8 * rows * NSTATE * chans,
        nbytes=16 * rows * chans,
    )


def attention(blocks, own_blocks, pieces, queries, grads, kv_heads):
    rows = queries.shape[0]
    per_kv = queries.shape[1] // AHD // kv_heads
    n_pieces = len(pieces)
    tokens = rows * sum(piece.shape[0] for piece in pieces)
    half_width = kv_heads * AHD
    scale = AHD ** (-0.5)
    chunk = min(KEY_CHUNK, tokens)
    tall = per_kv * STRETCH

    def kernel(*refs):
        blocks_ref, own_ref = refs[:2]
        piece_refs = refs[2 : 2 + n_pieces]
        q_ref, g_ref, out_ref, dq_ref, kv, scores, q_all, g_all = refs[2 + n_pieces :]
        index = 0
        for ref in piece_refs:
            for u in range(ref.shape[0]):
                for half in range(2):
                    at = pl.ds(pl.multiple_of(blocks_ref[half, index] * STRETCH, 64), STRETCH)
                    kv[at, :] = ref[u, half * STRETCH : (half + 1) * STRETCH, :]
                index += 1
        offset = lax.broadcasted_iota(jnp.int32, (tall, chunk), 0) % STRETCH
        column = lax.broadcasted_iota(jnp.int32, (tall, chunk), 1)
        every = range(kv_heads)
        k_at = [slice(g * AHD, (g + 1) * AHD) for g in every]
        v_at = [slice(half_width + g * AHD, half_width + (g + 1) * AHD) for g in every]

        def stacked(ref, src, g):
            parts = [ref[src, (g * per_kv + i) * AHD : (g * per_kv + i + 1) * AHD] for i in range(per_kv)]
            return jnp.concatenate(parts, axis=0)

        def keys_of(c):
            return pl.ds(pl.multiple_of(c * chunk, chunk), chunk)

        for half in range(2):
            block = own_ref[half]
            src = slice(half * STRETCH, (half + 1) * STRETCH)
            steps = (block * STRETCH) // chunk + 1
            reach = offset + block * STRETCH
            for g in every:
                q_all[g] = stacked(q_ref, src, g)
                g_all[g] = stacked(g_ref, src, g)

            def first(c, peaks):
                kept = column + c * chunk <= reach
                new = []
                for g in every:
                    value = mm_nt(q_all[g], kv[keys_of(c), k_at[g]]) * (scale * LOG2_E)
                    value = jnp.where(kept, value, NEG_FILL)
                    scores[g, c] = value
                    new.append(jnp.maximum(peaks[g], jnp.max(value, axis=1, keepdims=True)))
                return tuple(new)

            peaks = lax.fori_loop(
                0, steps, first, tuple(jnp.full((tall, 1), NEG_FILL, F32) for _ in every)
            )

            def second(c, carry):
                new = []
                for g in every:
                    total, out = carry[g]
                    value = jnp.exp2(scores[g, c] - peaks[g])
                    scores[g, c] = value
                    out = out + mm(value.astype(BF16), kv[keys_of(c), v_at[g]])
                    new.append((total + jnp.sum(value, axis=1, keepdims=True), out))
                return tuple(new)

            empty = (jnp.zeros((tall, 1), F32), jnp.zeros((tall, AHD), F32))
            done = lax.fori_loop(0, steps, second, tuple(empty for _ in every))
            deltas = []
            for g in every:
                total, out = done[g]
                out = (out / total).astype(BF16)
                deltas.append(
                    jnp.sum(g_all[g].astype(F32) * out.astype(F32), axis=1, keepdims=True)
                )
                for i in range(per_kv):
                    at = slice((g * per_kv + i) * AHD, (g * per_kv + i + 1) * AHD)
                    out_ref[src, at] = out[i * STRETCH : (i + 1) * STRETCH]

            def third(c, carry):
                new = []
                for g in every:
                    slope = mm_nt(g_all[g], kv[keys_of(c), v_at[g]]) - deltas[g]
                    change = (scores[g, c] * slope).astype(BF16)
                    new.append(carry[g] + mm(change, kv[keys_of(c), k_at[g]]))
                return tuple(new)

            changes = lax.fori_loop(
                0, steps, third, tuple(jnp.zeros((tall, AHD), F32) for _ in every)
            )
            for g in every:
                change = (changes[g] * (scale / done[g][0])).astype(BF16)
                for i in range(per_kv):
                    at = slice((g * per_kv + i) * AHD, (g * per_kv + i + 1) * AHD)
                    dq_ref[src, at] = change[i * STRETCH : (i + 1) * STRETCH]

    return call(
        kernel,
        [(queries.shape, BF16), (queries.shape, BF16)],
        (blocks, own_blocks, *pieces, queries, grads),
        smem=(0, 1),
        scratch=[
            pltpu.VMEM((tokens, 2 * half_width), BF16),
            pltpu.VMEM((kv_heads, tokens // chunk, tall, chunk), F32),
            pltpu.VMEM((kv_heads, tall, AHD), BF16),
            pltpu.VMEM((kv_heads, tall, AHD), BF16),
        ],
        mib=24,
        flops=10 * queries.size * tokens,
        nbytes=4 * tokens * half_width,
    )


def body(
    stretch_order,
    attn_queries,
    attn_keys,
    attn_values,
    attn_grad,
    mamba_input,
    gate_input,
    state_write,
    state_read,
    step_raw,
    decay_log,
    skip_gain,
    norm_gain,
    mamba_grad,
):
    ctx_count = lax.axis_size("ctx")
    tp_count = lax.axis_size("tp")
    group = state_write.shape[1] // NSTATE
    units = ctx_count // group
    by_permute = units <= 4
    my_index = lax.axis_index("ctx")
    my_unit, my_place = my_index // group, my_index % group
    me = my_place.astype(jnp.int32).reshape(1)
    chans = mamba_input.shape[1] // group
    heads = chans // HEAD_CH
    kv_heads = attn_keys.shape[1] // AHD
    turn = stretch_order[0]
    last = 2 * ctx_count

    def to_place(value, m):
        pairs = [(i, (i // group) * group + ((i % group) ^ m)) for i in range(ctx_count)]
        return lax.ppermute(value, "ctx", pairs)

    def in_plane(values):
        return [values[0]] + [to_place(values[m], m) for m in range(1, group)]

    def across(value):
        moved = []
        for m in range(units - 1, 0, -1):
            pairs = [(i, ((i // group) ^ m) * group + i % group) for i in range(ctx_count)]
            moved.append(lax.ppermute(value, "ctx", pairs))
        return [value] + moved[::-1]

    def all_units(value):
        if by_permute:
            return [part[None] for part in across(value)]
        if group == 1:
            return [lax.all_gather(value, "ctx", axis=0)]
        sets = [[u * group + j for u in range(units)] for j in range(group)]
        return [lax.all_gather(value, "ctx", axis=0, axis_index_groups=sets)]

    own_kv, packed = pack_forward(
        mamba_input, state_write, state_read, step_raw, attn_keys, attn_values, group
    )
    kv_units = all_units(own_kv)
    forward_pieces = packed
    if group > 1:
        planes = [[u * group + j for j in range(group)] for u in range(units)]
        forward_pieces = lax.all_to_all(packed, "ctx", 0, 0, axis_index_groups=planes, tiled=True)

    unit_ids = jnp.arange(units, dtype=jnp.int32)
    if by_permute:
        unit_ids = unit_ids ^ my_unit
    place_ids = jnp.arange(group, dtype=jnp.int32) ^ my_place

    def class_bounds(unit):
        first = (unit * group + turn) % ctx_count
        wraps = first + group > ctx_count
        extra = first + group - ctx_count
        out_start = (jnp.where(wraps, 0, first), jnp.where(wraps, first, last - first - group))
        out_end = (jnp.where(wraps, extra, first + group), last - first)
        in_start = (first, jnp.where(wraps, last - extra, last - first - group))
        in_end = (
            jnp.where(wraps, last - first, first + group),
            jnp.where(wraps, last, last - first),
        )
        return out_start, out_end, in_start, in_end

    out_start, out_end, in_start, in_end = class_bounds(my_unit)
    _, all_out_end, all_in_start, _ = class_bounds(unit_ids)
    all_out_end = jnp.stack(all_out_end, axis=1).reshape(-1)
    all_in_start = jnp.stack(all_in_start, axis=1).reshape(-1)
    own_out_end = jnp.stack(out_end)
    own_in_start = jnp.stack(in_start)
    enter_mask = (all_out_end[None, :] <= own_in_start[:, None]).astype(F32)
    leave_mask = (own_out_end[:, None] <= all_in_start[None, :]).astype(F32)
    own_end = (all_out_end[None, :] <= own_out_end[:, None]).astype(F32)
    before_in = (all_out_end[None, :] <= all_in_start[:, None]).astype(F32)
    ends = (all_out_end[None, :] <= all_out_end[:, None]).astype(F32)
    own_mask = jnp.concatenate([enter_mask, jnp.zeros((6, 2 * units), F32)], axis=0)
    own_end = jnp.concatenate([own_end, jnp.zeros((6, 2 * units), F32)], axis=0)

    def info_of(row):
        half, place, offset = row // (group * STRETCH), (row // STRETCH) % group, row % STRETCH
        pair = (my_unit * group + (place ^ my_place) + turn) % ctx_count
        block = jnp.where(half == 0, pair, last - 1 - pair)

        def within(start, end):
            return ((block >= start) & (block < end)).astype(F32)

        low = jnp.where(
            within(in_start[1], in_end[1]) > 0,
            in_start[1],
            jnp.where(within(in_start[0], in_end[0]) > 0, in_start[0], out_start[0]),
        )
        return [
            (block * STRETCH + offset).astype(F32),
            (low * STRETCH).astype(F32),
            within(out_start[0], out_end[0]),
            within(out_start[1], out_end[1]),
            within(in_start[0], in_end[0]),
            within(in_start[1], in_end[1]),
        ]

    rows = 2 * group * STRETCH
    cols = info_of(lax.broadcasted_iota(jnp.int32, (rows, 8), 0))
    pick = lax.broadcasted_iota(jnp.int32, (rows, 8), 1)
    info = sum(jnp.where(pick == i, c, 0.0) for i, c in enumerate(cols))
    cols = info_of(lax.broadcasted_iota(jnp.int32, (8, rows), 1))
    pick = lax.broadcasted_iota(jnp.int32, (8, rows), 0)
    info_t = sum(jnp.where(pick == i, c, 0.0) for i, c in enumerate(cols))

    decay = -jnp.exp(lax.dynamic_slice(decay_log, (my_place * heads,), (heads,)))
    small = jnp.pad(decay[None], ((0, 7), (0, 128 - heads)))
    skip = jnp.repeat(lax.dynamic_slice(skip_gain, (my_place * heads,), (heads,)), HEAD_CH)
    gain = lax.dynamic_slice(norm_gain, (my_place * chans,), (chans,))
    chan = jnp.pad(jnp.stack([skip, gain]), ((0, 6), (0, 0)))

    own_pair = (my_index + turn) % ctx_count
    pair_table = (unit_ids[None, :] * group + place_ids[:, None] + turn) % ctx_count
    pair_table = pair_table.reshape(1, -1)
    blocks = jnp.concatenate([pair_table, last - 1 - pair_table], axis=0)
    own_blocks = jnp.stack([own_pair, last - 1 - own_pair])
    tables = (
        info, info_t, small, chan, before_in, ends, enter_mask, leave_mask, own_mask, own_end,
        blocks, own_blocks,
    )
    small_group = group == 4 and units == 4 and by_permute
    gates = pack_gates(after(gate_input, (info, enter_mask, own_end)), mamba_grad, group)
    if group > 1:
        gates = lax.all_to_all(after(gates, forward_pieces), "ctx", 0, 0, axis_index_groups=planes, tiled=True)
    forward_pieces, tables = after((forward_pieces, tables), kv_units)
    (
        info, info_t, small, chan, before_in, ends, enter_mask, leave_mask, own_mask, own_end,
        blocks, own_blocks,
    ) = tables

    msg, x, w, r, cum, rate, tail = outgoing_state(me, forward_pieces, info, info_t, small, chans)
    msgs = all_units(msg)
    y = intra_forward(x, w, r, cum, rate, info, info_t, chan)
    if small_group:
        near = stack_parts(after(kv_units, (gates, y)))
        beside, above = to_place(near, 1), to_place(near, 2)
        x_late = x
    else:
        kv_pieces = in_plane([jnp.concatenate(kv_units, axis=0)] * group)
        x_late = x
    gated, sums, state, enter, leave = mixed_rows(
        me, msgs, y, r, cum, gates, info, chan, before_in, ends, enter_mask, own_mask, own_end
    )
    if tp_count == 2:
        sums = sums + lax.ppermute(sums, "tp", [(0, 1), (1, 0)])
    else:
        sums = lax.psum(sums, "tp")
    sums = in_plane([sums] * group)
    touch, dmix, lift, inv = mixed_cotangent(
        me, sums, gated, gates, r, cum, info_t, chan, float(mamba_input.shape[1] * tp_count)
    )
    touches = all_units(touch)
    if small_group:
        beside, above = after((beside, above), touch)
        kv_pieces = [near, beside, above, to_place(beside[:2], 2), to_place(above[2:], 1)]
    dx, dw, dr = intra_backward(x, w, r, cum, rate, dmix, lift, state, info, info_t)

    attn_output, query_grad = attention(
        blocks, own_blocks, kv_pieces, attn_queries, attn_grad, kv_heads
    )

    touches, attn_output, query_grad = lax.optimization_barrier((touches, attn_output, query_grad))
    finals = final_grads(
        touches, x, w, rate, tail, dx, dw, dr, dmix, gated, inv, info, chan, enter, leave, leave_mask
    )
    input_grad, write_grad, read_grad, mamba_output = unpack(
        me, in_plane(finals), (chans, NSTATE, NSTATE, chans)
    )
    return (attn_output, query_grad, mamba_output, input_grad, write_grad, read_grad)


def solution(mesh):
    wide, flat = P("ctx", "tp"), P("tp")
    return jax.shard_map(
        body,
        mesh=mesh,
        in_specs=(P(),) + (wide,) * 9 + (flat,) * 3 + (wide,),
        out_specs=(wide,) * 6,
        check_vma=False,
    )
```

```python
import jax
import jax.numpy as jnp
from jax import lax
from jax.experimental import pallas as pl
from jax.experimental.pallas import tpu as pltpu
from jax.sharding import PartitionSpec as P

HEAD_CH = 64
NSTATE = 128
AHD = 128
STRETCH = 64
EXTRA = 16
NORM_EPS = 1e-05
NEG_FILL = -1e30
KEY_CHUNK = 1024
LOG2_E = 1.4426950408889634
F32 = jnp.float32
BF16 = jnp.bfloat16
MIB = 1024 * 1024


def after(value, event):
    return lax.optimization_barrier((value, event))[0]


def mm(a, b):
    return lax.dot_general(a, b, (((1,), (0,)), ((), ())), preferred_element_type=F32)


def mm_nt(a, b):
    return lax.dot_general(a, b, (((1,), (1,)), ((), ())), preferred_element_type=F32)


def split3(v):
    hi = v.astype(BF16)
    rest = v - hi.astype(F32)
    mid = rest.astype(BF16)
    low = (rest - mid.astype(F32)).astype(BF16)
    return hi, mid, low


def pair_spread(cols, k):
    rows = cols.shape[0]
    lane = lax.broadcasted_iota(jnp.int32, (rows, 128), 1)
    even = jnp.broadcast_to(cols[:, 2 * k : 2 * k + 1], (rows, 128))
    odd = jnp.broadcast_to(cols[:, 2 * k + 1 : 2 * k + 2], (rows, 128))
    return jnp.where(lane < HEAD_CH, even, odd)


def spread(cols, heads):
    return jnp.concatenate([pair_spread(cols, k) for k in range(heads // 2)], axis=1)


def call(fn, outs, args, smem=(), scratch=(), flops=0, nbytes=0, mib=12):
    specs = [
        pl.BlockSpec(memory_space=pltpu.SMEM if i in smem else pltpu.VMEM)
        for i in range(len(args))
    ]
    return pl.pallas_call(
        fn,
        out_shape=tuple(jax.ShapeDtypeStruct(s, d) for s, d in outs),
        in_specs=specs,
        out_specs=tuple(pl.BlockSpec(memory_space=pltpu.VMEM) for _ in outs),
        scratch_shapes=list(scratch),
        compiler_params=pltpu.CompilerParams(vmem_limit_bytes=mib * MIB),
        cost_estimate=pl.CostEstimate(flops=flops // 1000, bytes_accessed=nbytes // 1000, transcendentals=0),
    )(*args)


def pack_gates(gate, grad, group):
    rows, chans = gate.shape[0], gate.shape[1] // group

    def kernel(gate_ref, grad_ref, out):
        for m in range(group):
            out[m, :, 0:chans] = gate_ref[:, m * chans : (m + 1) * chans]
            out[m, :, chans : 2 * chans] = grad_ref[:, m * chans : (m + 1) * chans]

    return call(kernel, [((group, rows, 2 * chans), BF16)], (gate, grad), nbytes=8 * gate.size)[0]


def pack_forward(x, w, r, step, keys, values, group):
    rows, chans = x.shape[0], x.shape[1] // group
    heads = step.shape[1] // group
    width = chans + 2 * NSTATE + 128
    kv_width = keys.shape[1]

    wide = [(0, chans), (1, NSTATE), (2, NSTATE), (None, 128)]
    sources = (x, w, r, keys, values)
    n_in = len(sources)
    n_out = 2 + group * len(wide)

    def kernel(step_ref, *refs):
        ins, kv_ref, out = refs[:n_in], *refs[n_in : n_in + 2]
        held = refs[n_in + 2 : -3]
        step_buf, in_sems, out_sems = refs[-3:]
        loads = [pltpu.make_async_copy(ins[i], held[i], in_sems.at[i]) for i in range(n_in)]
        for i in (3, 4, 0, 1, 2):
            loads[i].start()
        parts = split3(step_ref[...])
        row = lax.broadcasted_iota(jnp.int32, (heads * group, 128), 0)
        col = lax.broadcasted_iota(jnp.int32, (heads * group, 128), 1)
        for m in range(group):
            total = jnp.zeros((rows, 128), F32)
            for i in range(3):
                pick = (row - m * heads == col - i * heads) & (col >= i * heads)
                pick = pick & (col < (i + 1) * heads)
                total = total + mm(parts[i], jnp.where(pick, 1.0, 0.0).astype(BF16))
            step_buf[m] = total.astype(BF16)
        copies = []

        def send(src, dst):
            copy = pltpu.make_async_copy(src, dst, out_sems.at[len(copies)])
            copy.start()
            copies.append(copy)

        loads[3].wait()
        send(held[3], kv_ref.at[:, 0:kv_width])
        loads[4].wait()
        send(held[4], kv_ref.at[:, kv_width : 2 * kv_width])
        start = 0
        for source, count in wide:
            if source is not None:
                loads[source].wait()
            for m in range(group):
                at = slice(m * count, (m + 1) * count)
                dst = out.at[m, :, start : start + count]
                send(step_buf.at[m] if source is None else held[source].at[:, at], dst)
            start += count
        for copy in copies:
            copy.wait()

    return move(
        kernel,
        [((rows, 2 * kv_width), BF16)]
        + [((group, rows, width), BF16)],
        (step, *sources),
        (pltpu.VMEM,),
        [pltpu.VMEM(source.shape, BF16) for source in sources]
        + [
            pltpu.VMEM((group, rows, 128), BF16),
            pltpu.SemaphoreType.DMA((n_in,)),
            pltpu.SemaphoreType.DMA((n_out,)),
        ],
        mib=60,
    )


def move(fn, outs, args, spaces, scratch, mib=8):
    spaces = tuple(spaces) + (pl.ANY,) * (len(args) - len(spaces))
    return pl.pallas_call(
        fn,
        out_shape=tuple(jax.ShapeDtypeStruct(s, d) for s, d in outs),
        in_specs=[pl.BlockSpec(memory_space=space) for space in spaces],
        out_specs=tuple(pl.BlockSpec(memory_space=pl.ANY) for _ in outs),
        scratch_shapes=scratch,
        compiler_params=pltpu.CompilerParams(vmem_limit_bytes=mib * MIB),
        cost_estimate=pl.CostEstimate(flops=0, bytes_accessed=1024, transcendentals=0),
    )(*args)


def stack_parts(parts):
    count = len(parts)

    def kernel(*refs):
        for i in range(count):
            refs[count][i] = refs[i][0]

    shape = (count,) + parts[0].shape[1:]
    return call(kernel, [(shape, BF16)], parts, nbytes=4 * count * parts[0].size)[0]


def unpack(me, pieces, widths):
    group, rows = len(pieces), pieces[0].shape[0]

    def kernel(me_ref, *refs):
        outs = refs[group:]
        for m in range(group):
            start = 0
            for out, width in zip(outs, widths):
                at = pl.ds(pl.multiple_of((me_ref[0] ^ m) * width, 128), width)
                out[:, at] = refs[m][:, start : start + width]
                start += width

    return call(
        kernel,
        [((rows, group * width), BF16) for width in widths],
        (me, *pieces),
        smem=(0,),
        nbytes=4 * rows * group * sum(widths),
    )


def row_blocks(group):
    for half in range(2):
        for m in range(group):
            yield half, m, (half * group + m) * STRETCH


def outgoing_state(me, pieces, info, info_t, small, chans):
    group = pieces.shape[0]
    rows = 2 * group * STRETCH
    heads = chans // HEAD_CH

    def kernel(*refs):
        me_ref, ins, info_ref, info_t_ref, small_ref = refs[:5]
        msg, x_out, w_out, r_out, cum_out, rate_out, tail_out, step_buf = refs[5:]
        for half, m, at in row_blocks(group):
            src = slice(half * STRETCH, (half + 1) * STRETCH)
            x_out[at : at + STRETCH, :] = ins[me_ref[0] ^ m, src, 0:chans]
            w_out[at : at + STRETCH, :] = ins[me_ref[0] ^ m, src, chans : chans + NSTATE]
            r_out[at : at + STRETCH, :] = ins[me_ref[0] ^ m, src, chans + NSTATE : chans + 2 * NSTATE]
            step_buf[at : at + STRETCH, :] = ins[me_ref[0] ^ m, src, chans + 2 * NSTATE : chans + 2 * NSTATE + 128]
        row = lax.broadcasted_iota(jnp.int32, (128, 128), 0)
        col = lax.broadcasted_iota(jnp.int32, (128, 128), 1)
        pick = ((row == col) | (row == col + heads) | (row == col + 2 * heads)) & (col < heads)
        step = mm(step_buf[...], jnp.where(pick, 1.0, 0.0).astype(BF16))
        rate = jnp.maximum(step, 0.0) + jnp.log1p(jnp.exp(-jnp.abs(step)))
        rate_out[...] = rate
        amount = rate * small_ref[0:1, :]
        pos_row = info_t_ref[0:1, :]
        same = (pos_row <= info_ref[:, 0:1]) & (pos_row >= info_ref[:, 1:2])
        same = jnp.where(same, 1.0, 0.0).astype(BF16)
        hi, mid, low = split3(amount)
        cum = mm(same, hi) + mm(same, mid) + mm(same, low)
        cum_out[...] = cum
        totals = [
            jnp.sum(amount * info_ref[:, 2 + q : 3 + q], axis=0, keepdims=True) for q in range(2)
        ]
        tail = jnp.zeros_like(cum)
        for q in range(2):
            tail = tail + info_ref[:, 2 + q : 3 + q] * jnp.exp(jnp.minimum(totals[q] - cum, 0.0))
        tail_out[...] = tail
        scale = rate * tail
        w_t = w_out[...].astype(F32).T
        w_q = [(w_t * info_t_ref[2 + q : 3 + q, :]).astype(BF16) for q in range(2)]
        sub = lax.broadcasted_iota(jnp.int32, (EXTRA, 128), 0)
        for k in range(heads // 2):
            lanes = slice(128 * k, 128 * (k + 1))
            xw = (x_out[:, lanes].astype(F32) * pair_spread(scale, k)).astype(BF16)
            for q in range(2):
                msg[q * NSTATE : (q + 1) * NSTATE, lanes] = mm(w_q[q], xw).astype(BF16)
            picked = jnp.zeros((EXTRA, 128), F32)
            for q in range(2):
                wide = pair_spread(jnp.broadcast_to(totals[q], (EXTRA, 128)), k)
                for i, part in enumerate(split3(wide)):
                    picked = jnp.where(sub == 3 * q + i, part.astype(F32), picked)
            msg[2 * NSTATE :, lanes] = picked.astype(BF16)

    return call(
        kernel,
        [
            ((2 * NSTATE + EXTRA, chans), BF16),
            ((rows, chans), BF16),
            ((rows, NSTATE), BF16),
            ((rows, NSTATE), BF16),
            ((rows, 128), F32),
            ((rows, 128), F32),
            ((rows, 128), F32),
        ],
        (me, pieces, info, info_t, small),
        smem=(0,),
        scratch=[pltpu.VMEM((rows, 128), BF16)],
        flops=4 * rows * NSTATE * chans,
        nbytes=6 * rows * chans,
    )


def intra_forward(x, w, r, cum, rate, info, info_t, chan):
    rows, chans = x.shape
    heads = chans // HEAD_CH
    mid = rows // 2

    def kernel(x_ref, w_ref, r_ref, cum_ref, rate_ref, info_ref, info_t_ref, chan_ref, y_ref, gm):
        cum_t = cum_ref[...].T
        lane = lax.broadcasted_iota(jnp.int32, (mid, 128), 1)
        spans = ((0, mid, mid), (mid, mid, rows))
        for start, count, depth in spans:
            at = slice(start, start + count)
            pos_row = info_t_ref[0:1, 0:depth]
            same = (pos_row <= info_ref[at, 0:1]) & (pos_row >= info_ref[at, 1:2])
            gm[at, 0:depth] = jnp.where(same, mm_nt(r_ref[at, :], w_ref[0:depth, :]), 0.0)
        for k in range(heads // 2):
            lanes = slice(128 * k, 128 * (k + 1))
            xf = x_ref[:, lanes].astype(F32)
            xr = (xf * pair_spread(rate_ref[...], k)).astype(BF16)
            for start, count, depth in spans:
                at = slice(start, start + count)
                both = []
                for h in (2 * k, 2 * k + 1):
                    gap = cum_ref[at, h : h + 1] - cum_t[h : h + 1, 0:depth]
                    mix = (jnp.exp(jnp.minimum(gap, 0.0)) * gm[at, 0:depth]).astype(BF16)
                    both.append(mm(mix, xr[0:depth]))
                y_ref[at, lanes] = jnp.where(lane < HEAD_CH, both[0], both[1]) + (
                    chan_ref[0:1, lanes] * xf[at]
                )

    return call(
        kernel,
        [((rows, chans), F32)],
        (x, w, r, cum, rate, info, info_t, chan),
        scratch=[pltpu.VMEM((rows, rows), F32)],
        flops=4 * rows * rows * chans,
        nbytes=8 * rows * chans,
    )[0]


def gather_states(refs, weight, store):
    for q in range(2):
        total = None
        index = 0
        for ref in refs:
            for k in range(ref.shape[0]):
                for c in range(2):
                    term = weight(q, index) * ref[k, c * NSTATE : (c + 1) * NSTATE, :].astype(F32)
                    total = term if total is None else total + term
                    index += 1
        store(q, total)


def mixed_rows(me, msgs, y, r, cum, gates, info, chan, before_in, ends, enter_mask, own_mask, own_end):
    rows, chans = y.shape
    heads = chans // HEAD_CH
    group = gates.shape[0]
    n_msg = len(msgs)
    classes = ends.shape[0]
    gate_at, grad_at = slice(0, chans), slice(chans, 2 * chans)

    def kernel(*refs):
        me_ref, msg_refs, gate_ref = refs[0], refs[1 : n_msg + 1], refs[n_msg + 1]
        (
            y_ref, r_ref, cum_ref, info_ref, chan_ref,
            before_ref, ends_ref, own_ref, own_end_ref, mask_ref,
            gated_ref, sums_ref, state_ref, enter_ref, leave_ref,
            tot, inner, cols,
        ) = refs[n_msg + 2 :]
        index = 0
        for ref in msg_refs:
            for k in range(ref.shape[0]):
                part = ref[k, 2 * NSTATE :, :].astype(F32)
                for c in range(2):
                    tot[index : index + 1, :] = (
                        part[3 * c : 3 * c + 1]
                        + part[3 * c + 1 : 3 * c + 2]
                        + part[3 * c + 2 : 3 * c + 3]
                    )
                    index += 1
        exact = lax.Precision.HIGHEST
        totals = tot[...]
        enter_ref[...] = jnp.dot(before_ref[...], totals, precision=exact, preferred_element_type=F32)
        leave_all = jnp.dot(ends_ref[...], totals, precision=exact, preferred_element_type=F32)
        own_in = jnp.dot(own_ref[...], totals, precision=exact, preferred_element_type=F32)
        leave_ref[...] = jnp.dot(
            own_end_ref[...], totals, precision=exact, preferred_element_type=F32
        )

        def weight(q, c):
            gap = own_in[q : q + 1] - leave_all[c : c + 1]
            return jnp.exp(jnp.minimum(gap, 0.0)) * mask_ref[q, c]

        def store(q, value):
            state_ref[q * NSTATE : (q + 1) * NSTATE, :] = value.astype(BF16)

        gather_states(msg_refs, weight, store)
        reads = r_ref[...].astype(F32)
        both = jnp.concatenate(
            [(reads * info_ref[:, 4:5]).astype(BF16), (reads * info_ref[:, 5:6]).astype(BF16)], axis=1
        )
        inner[...] = mm(both, state_ref[...])
        lane = lax.broadcasted_iota(jnp.int32, (STRETCH, 128), 1)
        for half, m, at in row_blocks(group):
            here = slice(at, at + STRETCH)
            src = slice(half * STRETCH, (half + 1) * STRETCH)
            mixed = y_ref[here, :] + spread(jnp.exp(cum_ref[here, :]), heads) * inner[here, :]
            gate = gate_ref[me_ref[0] ^ m, src, gate_at].astype(F32)
            gated = mixed * (gate / (1.0 + jnp.exp(-gate)))
            gated_ref[here, :] = gated
            grad = gate_ref[me_ref[0] ^ m, src, grad_at].astype(F32) * chan_ref[1:2, :]
            square = jnp.sum(gated * gated, axis=1, keepdims=True)
            cross = jnp.sum(grad * gated, axis=1, keepdims=True)
            cols[here, :] = jnp.where(lane == 0, square, jnp.where(lane == 1, cross, 0.0))
        sums_ref[...] = cols[...].T[0:8, :]

    args = (
        me, *msgs, gates, y, r, cum, info, chan, before_in, ends, own_mask, own_end, enter_mask
    )
    return call(
        kernel,
        [
            ((rows, chans), F32),
            ((8, rows), F32),
            ((2 * NSTATE, chans), BF16),
            ((classes, chans), F32),
            ((8, chans), F32),
        ],
        args,
        smem=(0, len(args) - 1),
        scratch=[
            pltpu.VMEM((classes, chans), F32),
            pltpu.VMEM((rows, chans), F32),
            pltpu.VMEM((rows, 128), F32),
        ],
        flops=35 * 10**12,
        nbytes=16 * rows * chans,
    )


def mixed_cotangent(me, sums, gated, gates, r, cum, info_t, chan, total_chans):
    rows, chans = gated.shape
    heads = chans // HEAD_CH
    group = gates.shape[0]
    gate_at, grad_at = slice(0, chans), slice(chans, 2 * chans)

    def kernel(*refs):
        me_ref, gate_ref = refs[:2]
        sums_refs, refs = refs[2 : 2 + group], refs[2 + group :]
        gated_ref, r_ref, cum_ref, info_t_ref, chan_ref = refs[:5]
        touch_ref, dmix_ref, lift_ref, inv_ref, cols = refs[5:]
        parts = [ref[...] for ref in sums_refs]
        both = jnp.concatenate(parts + [jnp.zeros((128 - 8 * group, rows), F32)], axis=0)
        cols[...] = both.T
        for half, m, at in row_blocks(group):
            here = slice(at, at + STRETCH)
            src = slice(half * STRETCH, (half + 1) * STRETCH)
            square = cross = 0.0
            for peer in range(group):
                start = (half * group + (m ^ peer)) * STRETCH
                there = slice(start, start + STRETCH)
                square = square + cols[there, 8 * peer : 8 * peer + 1]
                cross = cross + cols[there, 8 * peer + 1 : 8 * peer + 2]
            inv = lax.rsqrt(square / total_chans + NORM_EPS)
            pull = inv * inv * inv * (cross / total_chans)
            gated = gated_ref[here, :]
            gain = chan_ref[1:2, :]
            inv_ref[here, :] = jnp.broadcast_to(inv, (STRETCH, 128))
            gate = gate_ref[me_ref[0] ^ m, src, gate_at].astype(F32)
            grad = gate_ref[me_ref[0] ^ m, src, grad_at].astype(F32) * gain
            dmix = (inv * grad - gated * pull) * (gate / (1.0 + jnp.exp(-gate)))
            dmix_ref[here, :] = dmix
            lift_ref[here, :] = (dmix * spread(jnp.exp(cum_ref[here, :]), heads)).astype(BF16)
        r_t = r_ref[...].astype(F32).T
        for q in range(2):
            left = (r_t * info_t_ref[4 + q : 5 + q, :]).astype(BF16)
            touch_ref[q * NSTATE : (q + 1) * NSTATE, :] = mm(left, lift_ref[...]).astype(BF16)

    return call(
        kernel,
        [
            ((2 * NSTATE, chans), BF16),
            ((rows, chans), F32),
            ((rows, chans), BF16),
            ((rows, 128), F32),
        ],
        (me, gates, *sums, gated, r, cum, info_t, chan),
        smem=(0,),
        scratch=[pltpu.VMEM((rows, 128), F32)],
        flops=4 * rows * NSTATE * chans,
        nbytes=16 * rows * chans,
    )


def intra_backward(x, w, r, cum, rate, dmix, lift, state, info, info_t):
    rows, chans = x.shape
    heads = chans // HEAD_CH
    mid = rows // 2

    def kernel(
        x_ref, w_ref, r_ref, cum_ref, rate_ref, dmix_ref, lift_ref, state_ref, info_ref, info_t_ref,
        dx_ref, dw_ref, dr_ref, gm, dgm,
    ):
        cum_t = cum_ref[...].T
        lane = lax.broadcasted_iota(jnp.int32, (rows, 128), 1)
        lane_mid = lax.broadcasted_iota(jnp.int32, (mid, 128), 1)
        spans = ((0, 0), (mid, mid))

        def same_of(start, later):
            pos = info_ref[start : start + mid, 0:1]
            return (pos <= info_t_ref[0:1, later:]) & (pos >= info_t_ref[1:2, later:])

        for start, later in spans:
            at = slice(start, start + mid)
            product = mm_nt(w_ref[at, :], r_ref[later:, :])
            gm[at, later:] = jnp.where(same_of(start, later), product, 0.0)
        for k in range(heads // 2):
            lanes = slice(128 * k, 128 * (k + 1))
            xr = x_ref[:, lanes].astype(F32) * pair_spread(rate_ref[...], k)
            parts = (
                jnp.where(lane < HEAD_CH, xr, 0.0).astype(BF16),
                jnp.where(lane < HEAD_CH, 0.0, xr).astype(BF16),
            )
            grads = dmix_ref[:, lanes].astype(BF16)
            for start, later in spans:
                at = slice(start, start + mid)
                both = []
                for i in range(2):
                    h = 2 * k + i
                    gap = cum_t[h : h + 1, later:] - cum_ref[at, h : h + 1]
                    fade = jnp.exp(jnp.minimum(gap, 0.0))
                    mix = (fade * gm[at, later:]).astype(BF16)
                    both.append(mm(mix, grads[later:]))
                    change = fade * mm_nt(parts[i][at], grads[later:])
                    if h == 0:
                        dgm[at, later:] = change
                    else:
                        dgm[at, later:] += change
                dx_ref[at, lanes] = jnp.where(lane_mid < HEAD_CH, both[0], both[1])
        carried = mm_nt(lift_ref[...], state_ref[0:NSTATE, :]) * info_ref[:, 4:5]
        carried = carried + mm_nt(lift_ref[...], state_ref[NSTATE:, :]) * info_ref[:, 5:6]
        dr_ref[...] = carried
        for start, later in spans:
            at = slice(start, start + mid)
            change = jnp.where(same_of(start, later), dgm[at, later:], 0.0)
            dw_ref[at, :] = mm(change.astype(BF16), r_ref[later:, :])
            dr_ref[later:, :] += mm(change.T.astype(BF16), w_ref[at, :])

    return call(
        kernel,
        [((rows, chans), F32), ((rows, NSTATE), F32), ((rows, NSTATE), F32)],
        (x, w, r, cum, rate, dmix, lift, state, info, info_t),
        scratch=[pltpu.VMEM((rows, rows), F32), pltpu.VMEM((rows, rows), F32)],
        flops=8 * rows * rows * chans,
        nbytes=16 * rows * chans,
    )


def final_grads(msgs, x, w, rate, tail, dx, dw, dr, dmix, gated, inv, info, chan, enter, leave, leave_mask):
    rows, chans = x.shape
    heads = chans // HEAD_CH
    group = rows // (2 * STRETCH)
    n_msg = len(msgs)
    width = 2 * chans + 2 * NSTATE

    def kernel(*refs):
        msg_refs = refs[:n_msg]
        (
            x_ref, w_ref, rate_ref, tail_ref, dx_ref, dw_ref, dr_ref, dmix_ref, gated_ref, inv_ref,
            info_ref, chan_ref, enter_ref, leave_ref, mask_ref,
        ) = refs[n_msg : n_msg + 15]
        outs = refs[n_msg + 15 : n_msg + 15 + group]
        after, inner, xw = refs[n_msg + 15 + group :]

        def weight(q, c):
            gap = enter_ref[c : c + 1, :] - leave_ref[q : q + 1, :]
            return jnp.exp(jnp.minimum(gap, 0.0)) * mask_ref[q, c]

        def store(q, value):
            after[q * NSTATE : (q + 1) * NSTATE, :] = value.astype(BF16)

        gather_states(msg_refs, weight, store)
        writes = w_ref[...].astype(F32)
        both = jnp.concatenate(
            [(writes * info_ref[:, 2:3]).astype(BF16), (writes * info_ref[:, 3:4]).astype(BF16)],
            axis=1,
        )
        inner[...] = mm(both, after[...])
        for half, m, at in row_blocks(group):
            here = slice(at, at + STRETCH)
            dst = slice(half * STRETCH, (half + 1) * STRETCH)
            rates = spread(rate_ref[here, :], heads)
            tails = spread(tail_ref[here, :], heads)
            xw[here, :] = (x_ref[here, :].astype(F32) * (rates * tails)).astype(BF16)
            change = rates * (dx_ref[here, :] + tails * inner[here, :])
            change = change + chan_ref[0:1, :] * dmix_ref[here, :]
            outs[m][dst, 0:chans] = change.astype(BF16)
            outs[m][dst, chans + NSTATE : chans + 2 * NSTATE] = dr_ref[here, :].astype(BF16)
            out = gated_ref[here, :] * inv_ref[here, 0:1] * chan_ref[1:2, :]
            outs[m][dst, chans + 2 * NSTATE :] = out.astype(BF16)
        change = dw_ref[...] + mm_nt(xw[...], after[0:NSTATE, :]) * info_ref[:, 2:3]
        change = change + mm_nt(xw[...], after[NSTATE:, :]) * info_ref[:, 3:4]
        for half, m, at in row_blocks(group):
            dst = slice(half * STRETCH, (half + 1) * STRETCH)
            outs[m][dst, chans : chans + NSTATE] = change[at : at + STRETCH].astype(BF16)

    args = (
        *msgs, x, w, rate, tail, dx, dw, dr, dmix, gated, inv, info, chan, enter, leave, leave_mask
    )
    return call(
        kernel,
        [((2 * STRETCH, width), BF16)] * group,
        args,
        smem=(len(args) - 1,),
        scratch=[
            pltpu.VMEM((2 * NSTATE, chans), BF16),
            pltpu.VMEM((rows, chans), F32),
            pltpu.VMEM((rows, chans), BF16),
        ],
        flops=8 * rows * NSTATE * chans,
        nbytes=16 * rows * chans,
    )


def attention(blocks, own_blocks, pieces, queries, grads, kv_heads):
    rows = queries.shape[0]
    per_kv = queries.shape[1] // AHD // kv_heads
    n_pieces = len(pieces)
    tokens = rows * sum(piece.shape[0] for piece in pieces)
    half_width = kv_heads * AHD
    scale = AHD ** (-0.5)
    chunk = min(KEY_CHUNK, tokens)
    tall = per_kv * STRETCH

    def kernel(*refs):
        blocks_ref, own_ref = refs[:2]
        piece_refs = refs[2 : 2 + n_pieces]
        q_ref, g_ref, out_ref, dq_ref, kv, scores, q_all, g_all = refs[2 + n_pieces :]
        every = range(kv_heads)
        k_at = [slice(g * AHD, (g + 1) * AHD) for g in every]
        v_at = [slice(half_width + 2 * g * AHD, half_width + (2 * g + 1) * AHD) for g in every]
        w_at = [slice(half_width + 2 * g * AHD, half_width + (2 * g + 2) * AHD) for g in every]
        for g in every:
            kv[:, half_width + (2 * g + 1) * AHD : half_width + (2 * g + 2) * AHD] = jnp.ones(
                (tokens, AHD), BF16
            )
        index = 0
        for ref in piece_refs:
            for u in range(ref.shape[0]):
                for half in range(2):
                    at = pl.ds(pl.multiple_of(blocks_ref[half, index] * STRETCH, 64), STRETCH)
                    rows_at = slice(half * STRETCH, (half + 1) * STRETCH)
                    kv[at, 0:half_width] = ref[u, rows_at, 0:half_width]
                    for g in range(kv_heads):
                        kv[at, v_at[g]] = ref[u, rows_at, half_width + g * AHD : half_width + (g + 1) * AHD]
                index += 1
        offset = lax.broadcasted_iota(jnp.int32, (tall, chunk), 0) % STRETCH
        column = lax.broadcasted_iota(jnp.int32, (tall, chunk), 1)

        def stacked(ref, src, g):
            parts = [ref[src, (g * per_kv + i) * AHD : (g * per_kv + i + 1) * AHD] for i in range(per_kv)]
            return jnp.concatenate(parts, axis=0)

        def keys_of(c):
            return pl.ds(pl.multiple_of(c * chunk, chunk), chunk)

        for half in range(2):
            block = own_ref[half]
            src = slice(half * STRETCH, (half + 1) * STRETCH)
            steps = (block * STRETCH) // chunk + 1
            reach = offset + block * STRETCH
            for g in every:
                q_all[g] = stacked(q_ref, src, g)
                g_all[g] = stacked(g_ref, src, g)

            def first(c, peaks):
                kept = column + c * chunk <= reach
                new = []
                for g in every:
                    value = mm_nt(q_all[g], kv[keys_of(c), k_at[g]]) * (scale * LOG2_E)
                    value = jnp.where(kept, value, NEG_FILL)
                    scores[g, c] = value
                    best = peaks[g]
                    for i in range(chunk // 128):
                        best = jnp.maximum(best, value[:, i * 128 : (i + 1) * 128])
                    new.append(best)
                return tuple(new)

            peaks = lax.fori_loop(
                0, steps, first, tuple(jnp.full((tall, 128), NEG_FILL, F32) for _ in every)
            )
            peaks = [jnp.max(peak, axis=1, keepdims=True) for peak in peaks]

            def second(c, carry):
                new = []
                for g in every:
                    value = jnp.exp2(scores[g, c] - peaks[g])
                    scores[g, c] = value
                    new.append(carry[g] + mm(value.astype(BF16), kv[keys_of(c), w_at[g]]))
                return tuple(new)

            empty = jnp.zeros((tall, 2 * AHD), F32)
            done = lax.fori_loop(0, steps, second, tuple(empty for _ in every))
            deltas = []
            for g in every:
                out = (done[g][:, :AHD] / done[g][:, AHD:]).astype(BF16)
                deltas.append(
                    jnp.sum(g_all[g].astype(F32) * out.astype(F32), axis=1, keepdims=True)
                )
                for i in range(per_kv):
                    at = slice((g * per_kv + i) * AHD, (g * per_kv + i + 1) * AHD)
                    out_ref[src, at] = out[i * STRETCH : (i + 1) * STRETCH]

            def third(c, carry):
                new = []
                for g in every:
                    slope = mm_nt(g_all[g], kv[keys_of(c), v_at[g]]) - deltas[g]
                    change = (scores[g, c] * slope).astype(BF16)
                    new.append(carry[g] + mm(change, kv[keys_of(c), k_at[g]]))
                return tuple(new)

            changes = lax.fori_loop(
                0, steps, third, tuple(jnp.zeros((tall, AHD), F32) for _ in every)
            )
            for g in every:
                change = (changes[g] * (scale / done[g][:, AHD:])).astype(BF16)
                for i in range(per_kv):
                    at = slice((g * per_kv + i) * AHD, (g * per_kv + i + 1) * AHD)
                    dq_ref[src, at] = change[i * STRETCH : (i + 1) * STRETCH]

    return call(
        kernel,
        [(queries.shape, BF16), (queries.shape, BF16)],
        (blocks, own_blocks, *pieces, queries, grads),
        smem=(0, 1),
        scratch=[
            pltpu.VMEM((tokens, 3 * half_width), BF16),
            pltpu.VMEM((kv_heads, tokens // chunk, tall, chunk), F32),
            pltpu.VMEM((kv_heads, tall, AHD), BF16),
            pltpu.VMEM((kv_heads, tall, AHD), BF16),
        ],
        mib=36,
        flops=10 * queries.size * tokens,
        nbytes=4 * tokens * half_width,
    )


def body(
    stretch_order,
    attn_queries,
    attn_keys,
    attn_values,
    attn_grad,
    mamba_input,
    gate_input,
    state_write,
    state_read,
    step_raw,
    decay_log,
    skip_gain,
    norm_gain,
    mamba_grad,
):
    ctx_count = lax.axis_size("ctx")
    tp_count = lax.axis_size("tp")
    group = state_write.shape[1] // NSTATE
    units = ctx_count // group
    by_permute = units <= 4
    my_index = lax.axis_index("ctx")
    my_unit, my_place = my_index // group, my_index % group
    me = my_place.astype(jnp.int32).reshape(1)
    chans = mamba_input.shape[1] // group
    heads = chans // HEAD_CH
    kv_heads = attn_keys.shape[1] // AHD
    turn = stretch_order[0]
    last = 2 * ctx_count

    def to_place(value, m):
        pairs = [(i, (i // group) * group + ((i % group) ^ m)) for i in range(ctx_count)]
        return lax.ppermute(value, "ctx", pairs)

    def in_plane(values):
        return [values[0]] + [to_place(values[m], m) for m in range(1, group)]

    def across(value):
        moved = []
        for m in range(units - 1, 0, -1):
            pairs = [(i, ((i // group) ^ m) * group + i % group) for i in range(ctx_count)]
            moved.append(lax.ppermute(value, "ctx", pairs))
        return [value] + moved[::-1]

    def all_units(value):
        if by_permute:
            return [part[None] for part in across(value)]
        if group == 1:
            return [lax.all_gather(value, "ctx", axis=0)]
        sets = [[u * group + j for u in range(units)] for j in range(group)]
        return [lax.all_gather(value, "ctx", axis=0, axis_index_groups=sets)]

    own_kv, packed = pack_forward(
        mamba_input, state_write, state_read, step_raw, attn_keys, attn_values, group
    )
    kv_units = all_units(own_kv)
    forward_pieces = packed
    if group > 1:
        planes = [[u * group + j for j in range(group)] for u in range(units)]
        forward_pieces = lax.all_to_all(packed, "ctx", 0, 0, axis_index_groups=planes, tiled=True)

    unit_ids = jnp.arange(units, dtype=jnp.int32)
    if by_permute:
        unit_ids = unit_ids ^ my_unit
    place_ids = jnp.arange(group, dtype=jnp.int32) ^ my_place

    def class_bounds(unit):
        first = (unit * group + turn) % ctx_count
        wraps = first + group > ctx_count
        extra = first + group - ctx_count
        out_start = (jnp.where(wraps, 0, first), jnp.where(wraps, first, last - first - group))
        out_end = (jnp.where(wraps, extra, first + group), last - first)
        in_start = (first, jnp.where(wraps, last - extra, last - first - group))
        in_end = (
            jnp.where(wraps, last - first, first + group),
            jnp.where(wraps, last, last - first),
        )
        return out_start, out_end, in_start, in_end

    out_start, out_end, in_start, in_end = class_bounds(my_unit)
    _, all_out_end, all_in_start, _ = class_bounds(unit_ids)
    all_out_end = jnp.stack(all_out_end, axis=1).reshape(-1)
    all_in_start = jnp.stack(all_in_start, axis=1).reshape(-1)
    own_out_end = jnp.stack(out_end)
    own_in_start = jnp.stack(in_start)
    enter_mask = (all_out_end[None, :] <= own_in_start[:, None]).astype(F32)
    leave_mask = (own_out_end[:, None] <= all_in_start[None, :]).astype(F32)
    own_end = (all_out_end[None, :] <= own_out_end[:, None]).astype(F32)
    before_in = (all_out_end[None, :] <= all_in_start[:, None]).astype(F32)
    ends = (all_out_end[None, :] <= all_out_end[:, None]).astype(F32)
    own_mask = jnp.concatenate([enter_mask, jnp.zeros((6, 2 * units), F32)], axis=0)
    own_end = jnp.concatenate([own_end, jnp.zeros((6, 2 * units), F32)], axis=0)

    def info_of(row):
        half, place, offset = row // (group * STRETCH), (row // STRETCH) % group, row % STRETCH
        pair = (my_unit * group + (place ^ my_place) + turn) % ctx_count
        block = jnp.where(half == 0, pair, last - 1 - pair)

        def within(start, end):
            return ((block >= start) & (block < end)).astype(F32)

        low = jnp.where(
            within(in_start[1], in_end[1]) > 0,
            in_start[1],
            jnp.where(within(in_start[0], in_end[0]) > 0, in_start[0], out_start[0]),
        )
        return [
            (block * STRETCH + offset).astype(F32),
            (low * STRETCH).astype(F32),
            within(out_start[0], out_end[0]),
            within(out_start[1], out_end[1]),
            within(in_start[0], in_end[0]),
            within(in_start[1], in_end[1]),
        ]

    rows = 2 * group * STRETCH
    cols = info_of(lax.broadcasted_iota(jnp.int32, (rows, 8), 0))
    pick = lax.broadcasted_iota(jnp.int32, (rows, 8), 1)
    info = sum(jnp.where(pick == i, c, 0.0) for i, c in enumerate(cols))
    cols = info_of(lax.broadcasted_iota(jnp.int32, (8, rows), 1))
    pick = lax.broadcasted_iota(jnp.int32, (8, rows), 0)
    info_t = sum(jnp.where(pick == i, c, 0.0) for i, c in enumerate(cols))

    decay = -jnp.exp(lax.dynamic_slice(decay_log, (my_place * heads,), (heads,)))
    small = jnp.pad(decay[None], ((0, 7), (0, 128 - heads)))
    skip = jnp.repeat(lax.dynamic_slice(skip_gain, (my_place * heads,), (heads,)), HEAD_CH)
    gain = lax.dynamic_slice(norm_gain, (my_place * chans,), (chans,))
    chan = jnp.pad(jnp.stack([skip, gain]), ((0, 6), (0, 0)))

    own_pair = (my_index + turn) % ctx_count
    pair_table = (unit_ids[None, :] * group + place_ids[:, None] + turn) % ctx_count
    pair_table = pair_table.reshape(1, -1)
    blocks = jnp.concatenate([pair_table, last - 1 - pair_table], axis=0)
    own_blocks = jnp.stack([own_pair, last - 1 - own_pair])
    tables = (
        info, info_t, small, chan, before_in, ends, enter_mask, leave_mask, own_mask, own_end,
        blocks, own_blocks,
    )
    small_group = group == 4 and units == 4 and by_permute
    gates = pack_gates(after(gate_input, (info, enter_mask, own_end)), mamba_grad, group)
    if group > 1:
        gates = lax.all_to_all(after(gates, forward_pieces), "ctx", 0, 0, axis_index_groups=planes, tiled=True)
    forward_pieces, tables = after((forward_pieces, tables), kv_units)
    (
        info, info_t, small, chan, before_in, ends, enter_mask, leave_mask, own_mask, own_end,
        blocks, own_blocks,
    ) = tables

    msg, x, w, r, cum, rate, tail = outgoing_state(me, forward_pieces, info, info_t, small, chans)
    msgs = all_units(msg)
    y = intra_forward(x, w, r, cum, rate, info, info_t, chan)
    if small_group:
        near = stack_parts(after(kv_units, (gates, y)))
        beside, above = to_place(near, 1), to_place(near, 2)
        x_late = x
    else:
        kv_pieces = in_plane([jnp.concatenate(kv_units, axis=0)] * group)
        x_late = x
    gated, sums, state, enter, leave = mixed_rows(
        me, msgs, y, r, cum, gates, info, chan, before_in, ends, enter_mask, own_mask, own_end
    )
    if tp_count == 2:
        sums = sums + lax.ppermute(sums, "tp", [(0, 1), (1, 0)])
    else:
        sums = lax.psum(sums, "tp")
    sums = in_plane([sums] * group)
    touch, dmix, lift, inv = mixed_cotangent(
        me, sums, gated, gates, r, cum, info_t, chan, float(mamba_input.shape[1] * tp_count)
    )
    touches = all_units(touch)
    if small_group:
        beside, above = after((beside, above), touch)
        kv_pieces = [near, beside, above, to_place(beside[:2], 2), to_place(above[2:], 1)]
    dx, dw, dr = intra_backward(x, w, r, cum, rate, dmix, lift, state, info, info_t)

    attn_output, query_grad = attention(
        blocks, own_blocks, kv_pieces, attn_queries, attn_grad, kv_heads
    )

    touches, attn_output, query_grad = lax.optimization_barrier((touches, attn_output, query_grad))
    finals = final_grads(
        touches, x, w, rate, tail, dx, dw, dr, dmix, gated, inv, info, chan, enter, leave, leave_mask
    )
    input_grad, write_grad, read_grad, mamba_output = unpack(
        me, in_plane(finals), (chans, NSTATE, NSTATE, chans)
    )
    return (attn_output, query_grad, mamba_output, input_grad, write_grad, read_grad)


def solution(mesh):
    wide, flat = P("ctx", "tp"), P("tp")
    return jax.shard_map(
        body,
        mesh=mesh,
        in_specs=(P(),) + (wide,) * 9 + (flat,) * 3 + (wide,),
        out_specs=(wide,) * 6,
        check_vma=False,
    )
```
